32 devices in a mesh: dp: 2 (over y), mp: 16 (over z, x, core).
Axes of the slice: x: 2, y: 2, z: 4, core: 2. Of those that a mesh axis runs over, the one named last changes fastest.
Arguments:
- queries: bfloat16 [2048, 4096], P('mp', 'dp'), may hold values from -200 to 200
- cache: bfloat16 [128, 128, 896], P('mp', 'dp'), may hold values from -6 to 6
- cache_scale: float32 [128, 128], P('mp', 'dp'), may hold values from 0.5 to 2
- w_kv: bfloat16 [2, 896, 2048], P(None, 'mp', 'dp'), may hold values from -0.1875 to 0.1875
- nbr_shard: int32 [64, 2], replicated, may hold values from 0 to 15, as said below
- nbr_row: int32 [64, 2], replicated, may hold values from 0 to 7
- grad_out: bfloat16 [2048, 4096], P('mp', 'dp'), may hold values from -6 to 6
Outputs:
- output: bfloat16 [2048, 4096], P('mp', 'dp')
- grad_queries: bfloat16 [2048, 4096], P('mp', 'dp')
The draws below stay inside these ranges and needn't reach their ends.
Inputs may be any that keep to these rules, and one draw needn't show every extreme that they name: `nbr_shard`: span c belongs to device c // 2 in dp-major order. Among the 2 * 2 * 2 requests of the spans whose devices share one mp index, no shard is named more than 2 times, and some shard exactly 2 times.
All inputs are finite; a program needn't handle non-finite values.
Results may differ from the reference program's by a relative error of at most 0.012.
The reference program's roundings to bfloat16 on the way (of `neighbours`, `probs_low` and `dscores`) count: a program that leaves them out, or rounds other values in their place, can miss the bound.
Values may be sent and summed in bfloat16 or wider, within the bound.
No kernel may reach another device: no remote copies, remote signals or barrier semaphores. Data moves between devices by JAX's collectives and lax.ppermute only.
A program may use at most 64 MiB of HBM per device.

```python
import math
import jax
import jax.numpy as jnp
from jax import lax

HEADS = 16
HEAD_DIM = 128
E = 896
NT = 128
SPAN = 64
NBR = 2
CH_DEV = 2
DB_DEV = 8
MOST = 2
DQ = 2048
TOKENS = 4096
SPANS = 64
DBROWS = 128
N_DP = 2
N_MP = 16


def draw_queries(key, part):
    key = jax.random.fold_in(key, 11)
    base_key = jax.random.fold_in(key, 0)
    values = jnp.clip(jax.random.normal(base_key, (DQ, TOKENS), jnp.float32), -6.0, 6.0)
    return values.astype(jnp.bfloat16)


def draw_nbr_shard(key, part):
    key = jax.random.fold_in(key, 5)
    hot_key, lead_key, noise_key, shuffle_key = jax.random.split(key, 4)
    vocabulary_count = N_MP * MOST
    block_size = N_DP * CH_DEV * NBR
    frequent_partition = jax.random.randint(hot_key, (N_MP,), 0, 4) == 0
    first_partition = jax.random.randint(lead_key, (N_MP,), 0, N_MP)
    gaussian_perturbation = jax.random.randint(noise_key, (N_MP, vocabulary_count), 0, 1024)
    holder_partition = jnp.arange(vocabulary_count, dtype=jnp.int32) // MOST
    surplus_increment = jnp.where(frequent_partition[holder_partition], 1024, 0)[None, :] + jnp.where(holder_partition[None, :] == first_partition[:, None], 4096, 0)
    affinity_logits = (gaussian_perturbation + surplus_increment) * vocabulary_count + jnp.arange(vocabulary_count, dtype=jnp.int32)[None, :]
    chosen = lax.top_k(affinity_logits, block_size)[1]
    picked = holder_partition[chosen]
    sub_keys = jax.random.split(shuffle_key, N_MP)
    shuffled = jax.vmap(lambda sub_key, picks: jax.random.permutation(sub_key, picks))(sub_keys, picked)
    arranged = shuffled.reshape(N_MP, N_DP, CH_DEV, NBR).transpose(1, 0, 2, 3)
    return arranged.reshape(SPANS, NBR).astype(jnp.int32)


def with_ends(values, stream_key, least, top_value):
    longest = values.shape.index(max(values.shape))
    spots = []
    for shift in (0, 1):
        where = [jax.random.randint(jax.random.fold_in(stream_key, axis), (), 0, length) for axis, length in enumerate(values.shape)]
        where[longest] = (where[longest] + shift) % values.shape[longest]
        spots.append(tuple(where))
    return values.at[spots[0]].set(least).at[spots[1]].set(top_value)


def levels(key, shape, pieces, smallest, top_value):
    level, own = 1.0, jax.random.fold_in(key, 6)
    for dim, parts in pieces:
        steps = jnp.exp(jax.random.uniform(jax.random.fold_in(own, dim), (parts,), jnp.float32, smallest / len(pieces), top_value / len(pieces)))
        level = level * jnp.repeat(steps, shape[dim] // parts).reshape([-1 if axis == dim else 1 for axis in range(len(shape))])
    return level


def normal_values(key, shape, width, limit, cuts=(), kind=jnp.bfloat16):
    gain = levels(key, shape, cuts, -0.22, 0.18) if cuts else 1.0
    entries = jax.random.normal(key, shape, jnp.float32) * width * gain
    return jnp.minimum(jnp.maximum(entries, -limit), limit).astype(kind)


def setup_inputs(seed: int = 0) -> dict:
    arg_keys = jax.random.split(jax.random.key(seed), 8)
    queries = draw_queries(jax.random.fold_in(arg_keys[7], 71), 0)
    cache = normal_values(arg_keys[1], (DBROWS, NT, E), 1.0, 6.0, ((0, 16), (1, 2)))
    cache_scale = jnp.clip(jnp.exp(math.log(2.0) - 1.3862944 * jax.random.uniform(arg_keys[2], (DBROWS, NT), jnp.float32) ** levels(arg_keys[2], (DBROWS, NT), ((0, 16), (1, 2)), -0.2, 0.2)), 0.5, 2.0)
    w_kv = normal_values(arg_keys[3], (2, E, DQ), E ** -0.5, 0.1875, ((1, 16), (2, 2)))
    nbr_shard = draw_nbr_shard(jax.random.fold_in(arg_keys[7], 71), 0)
    nbr_row = with_ends(jax.random.randint(arg_keys[5], (SPANS, NBR), 0, DB_DEV), jax.random.fold_in(arg_keys[5], 1), 0, DB_DEV - 1).astype(jnp.int32)
    grad_out = normal_values(arg_keys[6], (DQ, TOKENS), 1.0, 6.0, ((0, 16), (1, 2)))
    return dict(queries=queries, cache=cache, cache_scale=cache_scale, w_kv=w_kv, nbr_shard=nbr_shard, nbr_row=nbr_row, grad_out=grad_out)


def reference(queries, cache, cache_scale, w_kv, nbr_shard, nbr_row, grad_out):
    score_scale = HEAD_DIM ** -0.5
    groups = SPANS // CH_DEV
    query_blocks = queries.T.reshape(groups, CH_DEV, SPAN, HEADS, HEAD_DIM)
    grad_blocks = grad_out.T.reshape(groups, CH_DEV, SPAN, HEADS, HEAD_DIM)
    row_ids = (nbr_shard * DB_DEV + nbr_row).astype(jnp.int32).reshape(groups, CH_DEV, NBR)

    def one_group(operands):
        query_c, grad_c, group_rows = operands
        encoded = cache[group_rows].astype(jnp.float32)
        scales = cache_scale[group_rows].astype(jnp.float32)
        neighbours = (encoded * scales[..., None]).astype(jnp.bfloat16).reshape(CH_DEV, NBR * NT, E)
        key_value = jnp.einsum('cte,ken->kctn', neighbours.astype(jnp.float32), w_kv.astype(jnp.float32)).astype(jnp.bfloat16)
        key_rows = key_value[0].reshape(CH_DEV, NBR * NT, HEADS, HEAD_DIM)
        values = key_value[1].reshape(CH_DEV, NBR * NT, HEADS, HEAD_DIM)
        affinity_logits = jnp.einsum('cqhd,ckhd->chqk', query_c.astype(jnp.float32), key_rows.astype(jnp.float32)) * score_scale
        row_max = jnp.max(affinity_logits, axis=3, keepdims=True)
        exponent = jnp.exp(affinity_logits - row_max)
        attn_probs = exponent / jnp.sum(exponent, axis=3, keepdims=True)
        probs_low = attn_probs.astype(jnp.bfloat16)
        output = jnp.einsum('chqk,ckhd->cqhd', probs_low.astype(jnp.float32), values.astype(jnp.float32)).astype(jnp.bfloat16)
        dprobs = jnp.einsum('cqhd,ckhd->chqk', grad_c.astype(jnp.float32), values.astype(jnp.float32))
        row_delta = jnp.einsum('cqhd,cqhd->chq', grad_c.astype(jnp.float32), output.astype(jnp.float32))
        dscores = (attn_probs * (dprobs - row_delta[..., None]) * score_scale).astype(jnp.bfloat16)
        grad_query = jnp.einsum('chqk,ckhd->cqhd', dscores.astype(jnp.float32), key_rows.astype(jnp.float32)).astype(jnp.bfloat16)
        return output, grad_query

    output, grad_query = lax.map(one_group, (query_blocks, grad_blocks, row_ids))
    return output.reshape(TOKENS, DQ).T, grad_query.reshape(TOKENS, DQ).T
```

```python
import jax
import jax.numpy as jnp
from jax import lax
from jax.sharding import PartitionSpec as P

HEADS = 16
HEAD_DIM = 128
E = 896
NT = 128
SPAN = 64
NBR = 2
CH_DEV = 2


def shards(queries, cache, cache_scale, w_kv, nbr_shard, nbr_row, grad_out):
    dp_count = lax.axis_size("dp")
    mp_count = lax.axis_size("mp")
    my_mp = lax.axis_index("mp")
    slice_len = cache.shape[1]
    most_slots = 2 * ((dp_count * CH_DEV * NBR + mp_count - 1) // mp_count)
    block_size = dp_count * CH_DEV * NBR
    score_scale = HEAD_DIM ** (-0.5)
    local_query = lax.all_to_all(queries, "mp", split_axis=1, concat_axis=0, tiled=True)
    shard_blk = (
        nbr_shard.reshape(dp_count, mp_count, CH_DEV * NBR)
        .transpose(1, 0, 2)
        .reshape(mp_count, block_size)
    )
    row_blk = (
        nbr_row.reshape(dp_count, mp_count, CH_DEV * NBR)
        .transpose(1, 0, 2)
        .reshape(mp_count, block_size)
    )
    positions = jnp.arange(block_size, dtype=jnp.int32)
    earlier = positions[None, :] < positions[:, None]
    same_shard = shard_blk[:, :, None] == shard_blk[:, None, :]
    slot_blk = jnp.sum(jnp.logical_and(same_shard, earlier[None]), axis=2)
    to_me = shard_blk == my_mp
    slot_ids = jnp.arange(most_slots, dtype=jnp.int32)
    select = jnp.logical_and(to_me[:, None, :], slot_blk[:, None, :] == slot_ids[None, :, None])
    wanted = jnp.sum(jnp.where(select, row_blk[:, None, :], 0), axis=2)
    sending = (cache[wanted].astype(jnp.float32) * cache_scale[wanted][..., None]).astype(
        jnp.bfloat16
    )
    arrived = lax.all_to_all(sending, "mp", split_axis=0, concat_axis=0, tiled=True)
    flat_pieces = arrived.reshape(mp_count * most_slots, slice_len, E)
    own_shards = lax.dynamic_index_in_dim(shard_blk, my_mp, 0, keepdims=False)
    own_slots = lax.dynamic_index_in_dim(slot_blk, my_mp, 0, keepdims=False)
    pieces = jnp.take(flat_pieces, own_shards * most_slots + own_slots, axis=0)
    pieces = pieces.reshape(dp_count, CH_DEV * NBR, slice_len, E)
    gathered = lax.all_to_all(pieces, "dp", split_axis=0, concat_axis=2, tiled=True)
    neighbours = gathered.reshape(CH_DEV, NBR * NT, E)
    gathered_weights = lax.all_gather(w_kv, ("dp", "mp"), axis=0, tiled=False)
    all_weights = (
        gathered_weights.reshape((dp_count, mp_count) + w_kv.shape)
        .transpose(2, 1, 3, 0, 4)
        .reshape(2, E, HEADS * HEAD_DIM)
    )
    key_value = jnp.einsum(
        "cte,ken->kctn", neighbours, all_weights, preferred_element_type=jnp.float32
    ).astype(jnp.bfloat16)
    key_rows = key_value[0].reshape(CH_DEV, NBR * NT, HEADS, HEAD_DIM)
    values = key_value[1].reshape(CH_DEV, NBR * NT, HEADS, HEAD_DIM)
    query_c = local_query.reshape(HEADS, HEAD_DIM, CH_DEV, SPAN)
    affinity_logits = (
        jnp.einsum("hdcq,ckhd->chqk", query_c, key_rows, preferred_element_type=jnp.float32)
        * score_scale
    )
    row_max = jnp.max(affinity_logits, axis=3, keepdims=True)
    exponent = jnp.exp(affinity_logits - row_max)
    attn_probs = exponent / jnp.sum(exponent, axis=3, keepdims=True)
    probs_low = attn_probs.astype(jnp.bfloat16)
    output_c = jnp.einsum(
        "chqk,ckhd->hdcq", probs_low, values, preferred_element_type=jnp.float32
    ).astype(jnp.bfloat16)
    output_rows = output_c.reshape(HEADS * HEAD_DIM, CH_DEV * SPAN)
    output_back = lax.all_to_all(output_rows, "mp", split_axis=0, concat_axis=1, tiled=True)
    local_grad = lax.all_to_all(grad_out, "mp", split_axis=1, concat_axis=0, tiled=True)
    grad_c = local_grad.reshape(HEADS, HEAD_DIM, CH_DEV, SPAN)
    dprobs = jnp.einsum("hdcq,ckhd->chqk", grad_c, values, preferred_element_type=jnp.float32)
    row_delta = jnp.einsum("hdcq,hdcq->chq", grad_c, output_c, preferred_element_type=jnp.float32)
    dscores = (attn_probs * (dprobs - row_delta[..., None]) * score_scale).astype(jnp.bfloat16)
    grad_query = jnp.einsum(
        "chqk,ckhd->hdcq", dscores, key_rows, preferred_element_type=jnp.float32
    ).astype(jnp.bfloat16)
    grad_rows = grad_query.reshape(HEADS * HEAD_DIM, CH_DEV * SPAN)
    grad_back = lax.all_to_all(grad_rows, "mp", split_axis=0, concat_axis=1, tiled=True)
    return (output_back, grad_back)


def solution(mesh):
    return jax.shard_map(
        shards,
        mesh=mesh,
        in_specs=(
            P("mp", "dp"),
            P("mp", "dp", None),
            P("mp", "dp"),
            P(None, "mp", "dp"),
            P(),
            P(),
            P("mp", "dp"),
        ),
        out_specs=(P("mp", "dp"), P("mp", "dp")),
        check_vma=False,
    )
```

```python
import jax
import jax.numpy as jnp
from jax import lax
from jax.experimental import pallas as pl
from jax.experimental.pallas import tpu as pltpu
from jax.sharding import PartitionSpec as P

HEADS = 16
HEAD_DIM = 128
E = 896
NT = 128
SPAN = 64
NBR = 2
CH_DEV = 2
MOST = 2

SCORE_SCALE = HEAD_DIM ** (-0.5)


def requests(nbr_shard, nbr_row, dp_count, mp_count):
    block_size = dp_count * CH_DEV * NBR
    shard_blk = (
        nbr_shard.reshape(dp_count, mp_count, CH_DEV * NBR)
        .transpose(1, 0, 2)
        .reshape(mp_count, block_size)
    )
    row_blk = (
        nbr_row.reshape(dp_count, mp_count, CH_DEV * NBR)
        .transpose(1, 0, 2)
        .reshape(mp_count, block_size)
    )
    positions = jnp.arange(block_size, dtype=jnp.int32)
    earlier = positions[None, :] < positions[:, None]
    same_shard = shard_blk[:, :, None] == shard_blk[:, None, :]
    slot_blk = jnp.sum(jnp.logical_and(same_shard, earlier[None]), axis=2)
    return shard_blk, row_blk, slot_blk


ZS, XS, CS = 4, 2, 2
CHIPS = ZS * XS
HALF = 8
ALL = range(ZS * XS * CS)


def rows_kernel(rows_ref, src_ref, *refs):
    outs, sem = refs[:-1], refs[-1]
    copies = []
    for k in range(HALF):
        for s in range(MOST):
            copies.append(
                pltpu.make_async_copy(
                    src_ref.at[rows_ref[k * MOST + s]], outs[k].at[s], sem.at[k * MOST + s]
                )
            )
    for copy in copies:
        copy.start()
    for copy in copies:
        copy.wait()


def pick_rows(rows, source):
    piece = jax.ShapeDtypeStruct((MOST,) + source.shape[1:], source.dtype)
    return pl.pallas_call(
        rows_kernel,
        in_specs=[
            pl.BlockSpec(memory_space=pltpu.SMEM),
            pl.BlockSpec(memory_space=pl.ANY),
        ],
        out_specs=[pl.BlockSpec(memory_space=pl.ANY)] * HALF,
        out_shape=[piece] * HALF,
        scratch_shapes=[pltpu.SemaphoreType.DMA((HALF * MOST,))],
        name="pick_rows",
    )(rows, source)


def choose_kernel(where_ref, *refs):
    count = 2 * HALF
    pieces, outs, sem = refs[:count], refs[count:-1], refs[-1]
    for r in range(2 * CH_DEV * NBR):
        out = outs[r // (CH_DEV * NBR)].at[r % (CH_DEV * NBR)]
        piece, slot = where_ref[2 * r], where_ref[2 * r + 1]
        for p in range(count):

            @pl.when(piece == p)
            def _():
                pltpu.make_async_copy(pieces[p].at[slot], out, sem.at[r]).start()

    for r in range(2 * CH_DEV * NBR):
        out = outs[r // (CH_DEV * NBR)].at[r % (CH_DEV * NBR)]
        pltpu.make_async_copy(pieces[0].at[0], out, sem.at[r]).wait()


def choose(where, pieces):
    half = jax.ShapeDtypeStruct((CH_DEV * NBR,) + pieces[0].shape[1:], pieces[0].dtype)
    return pl.pallas_call(
        choose_kernel,
        in_specs=[pl.BlockSpec(memory_space=pltpu.SMEM)]
        + [pl.BlockSpec(memory_space=pl.ANY)] * len(pieces),
        out_specs=[pl.BlockSpec(memory_space=pl.ANY)] * 2,
        out_shape=[half] * 2,
        scratch_shapes=[pltpu.SemaphoreType.DMA((2 * CH_DEV * NBR,))],
        name="choose",
    )(where, *pieces)


def tdot(a, b):
    return lax.dot_general(a, b, (((0,), (0,)), ((), ())), preferred_element_type=jnp.float32)


def ndot(a, b):
    return jnp.dot(a, b, preferred_element_type=jnp.float32)


def attend_kernel(
    place_ref, na, nb, sa, sb, k0, kx, ky, kd, v0, vx, vy, vd, qg_ref, out_ref, n_scr, w_scr
):
    step = pl.program_id(0)
    d_heads = HEADS // CS // 2
    my_c, my_z, my_x = place_ref[1], place_ref[2], place_ref[3]
    rows = w_scr.shape[0] // CHIPS

    @pl.when(step == 0)
    def _():
        for s in range(CH_DEV):
            for core, first, second in ((my_c, na, nb), (1 - my_c, sa, sb)):
                n_scr[CH_DEV * core + s, 0:NT, :] = first[s]
                n_scr[CH_DEV * core + s, NT : 2 * NT, :] = second[s]

    def put(own, other, lane):
        for r in range(ZS):
            src_z = lax.rem(my_z - r + ZS, ZS)
            for x_at, ref in ((my_x, own), (1 - my_x, other)):
                at = pl.multiple_of((src_z * XS + x_at) * rows, 16)
                w_scr[pl.ds(at, rows), lane : lane + HEAD_DIM] = ref[r]

    @pl.when(step < d_heads)
    def _():
        put(k0, kx, 0)
        put(v0, vx, HEAD_DIM)

    @pl.when(step >= d_heads)
    def _():
        put(ky, kd, 0)
        put(vy, vd, HEAD_DIM)

    keys = NBR * NT
    weights = w_scr[...]
    lane = lax.broadcasted_iota(jnp.int32, (1, 2 * SPAN), 1)
    low = lane < SPAN
    for p in range(CS):
        kv = [
            ndot(n_scr[CH_DEV * p + s], weights).astype(jnp.bfloat16) for s in range(CH_DEV)
        ]
        ka, kb = kv[0][:, :HEAD_DIM], kv[1][:, :HEAD_DIM]
        va, vb = kv[0][:, HEAD_DIM:], kv[1][:, HEAD_DIM:]
        at = slice(2 * SPAN * p, 2 * SPAN * (p + 1))
        q = qg_ref[0, 0, :, at]
        g = qg_ref[0, 1, :, at]
        scores = jnp.where(low, ndot(ka, q), ndot(kb, q)) * SCORE_SCALE
        exponent = jnp.exp(scores - jnp.max(scores, axis=0, keepdims=True))
        probs = exponent / jnp.sum(exponent, axis=0, keepdims=True)
        probs_low = probs.astype(jnp.bfloat16)
        out = jnp.where(low, tdot(va, probs_low), tdot(vb, probs_low)).astype(jnp.bfloat16)
        dprobs = jnp.where(low, ndot(va, g), ndot(vb, g))
        delta = jnp.sum(
            g.astype(jnp.float32) * out.astype(jnp.float32), axis=0, keepdims=True
        )
        dscores = (probs * (dprobs - delta) * SCORE_SCALE).astype(jnp.bfloat16)
        dq = jnp.where(low, tdot(ka, dscores), tdot(kb, dscores)).astype(jnp.bfloat16)
        out_ref[0, 0, :, at] = out
        out_ref[0, 1, :, at] = dq


def attend(place, neighbours, weights, qg):
    d_heads = HEADS // CS // 2
    heads = 2 * d_heads
    tokens = qg.shape[-1]

    def whole(a):
        return pl.BlockSpec(a.shape, lambda i, place: (0,) * a.ndim)

    def own(a):
        return pl.BlockSpec(
            a.shape[:2] + (HEAD_DIM,), lambda i, place: (0, 0, jnp.minimum(i, d_heads - 1))
        )

    def other(a):
        return pl.BlockSpec(
            a.shape[:2] + (HEAD_DIM,), lambda i, place: (0, 0, jnp.maximum(i - d_heads, 0))
        )

    head_block = pl.BlockSpec(
        (1, 2, HEAD_DIM, tokens),
        lambda i, place: (lax.rem(i + d_heads * place[0], heads), 0, 0, 0),
    )
    return pl.pallas_call(
        attend_kernel,
        grid_spec=pltpu.PrefetchScalarGridSpec(
            num_scalar_prefetch=1,
            grid=(heads,),
            in_specs=[whole(a) for a in neighbours]
            + [f(a) for f, a in zip((own, own, other, other) * 2, weights)]
            + [head_block],
            out_specs=head_block,
            scratch_shapes=[
                pltpu.VMEM((CS * CH_DEV, NBR * NT, E), jnp.bfloat16),
                pltpu.VMEM((E, 2 * HEAD_DIM), jnp.bfloat16),
            ],
        ),
        out_shape=jax.ShapeDtypeStruct(qg.shape, jnp.bfloat16),
        compiler_params=pltpu.CompilerParams(vmem_limit_bytes=40 * 1024 * 1024),
        name="attend",
    )(place, *neighbours, *weights, qg)


def small(queries, cache, cache_scale, w_kv, nbr_shard, nbr_row, grad_out):
    dp_count = lax.axis_size("dp")
    mp_count = lax.axis_size("mp")
    my_dp = lax.axis_index("dp")
    my_mp = lax.axis_index("mp")
    my_c, my_x, my_z = my_mp & 1, (my_mp >> 1) & 1, my_mp >> 2
    place = jnp.stack([my_dp, my_c, my_z, my_x]).astype(jnp.int32)
    slice_len = cache.shape[1]
    e_loc = w_kv.shape[1]

    def swap(a, bits):
        return lax.ppermute(a, "mp", [(m, m ^ bits) for m in ALL])

    def swap_dp(a):
        return lax.ppermute(a, "dp", [(0, 1), (1, 0)])

    by_parity = w_kv.reshape(2, e_loc, -1, CS, HEAD_DIM)
    mine = lax.dynamic_index_in_dim(by_parity, my_c, 3, keepdims=False).reshape(2, e_loc, -1)
    sends = lax.dynamic_index_in_dim(by_parity, 1 - my_c, 3, keepdims=False).reshape(2, e_loc, -1)
    came = swap(sends, 1)
    first = my_c == 0
    chip_w = jnp.concatenate(
        [jnp.where(first, mine, came), jnp.where(first, came, mine)], axis=1
    )

    scaled = (cache.astype(jnp.float32) * cache_scale[..., None]).astype(jnp.bfloat16)
    far = swap(scaled, HALF)
    shard_blk, row_blk, slot_blk = requests(nbr_shard, nbr_row, dp_count, mp_count)
    holders = jnp.stack([my_mp, my_mp ^ HALF]).astype(jnp.int32)
    takers = my_mp ^ jnp.arange(HALF, dtype=jnp.int32)
    select = jnp.logical_and(
        shard_blk[:, None, None, :] == holders[None, :, None, None],
        slot_blk[:, None, None, :] == jnp.arange(MOST, dtype=jnp.int32)[None, None, :, None],
    )
    wanted = jnp.sum(jnp.where(select, row_blk[:, None, None, :], 0), axis=3)[takers]
    near_pieces = pick_rows(wanted[:, 0].reshape(-1), scaled)
    near_pieces = [near_pieces[0]] + [swap(near_pieces[k], k) for k in range(1, HALF)]

    turned = [chip_w] + [
        lax.ppermute(chip_w, "mp", [(m, (m + XS * CS * r) % len(ALL)) for m in ALL])
        for r in range(1, ZS)
    ]
    k0 = jnp.stack([t[0] for t in turned])
    v0 = jnp.stack([t[1] for t in turned])
    kx, vy = swap(k0, CS), swap_dp(v0)
    vx, ky = swap(v0, CS), swap_dp(k0)
    vd, kd = swap(vy, CS), swap_dp(kx)

    far_pieces = pick_rows(wanted[:, 1].reshape(-1), far)
    far_pieces = [far_pieces[0]] + [swap(far_pieces[k], k) for k in range(1, HALF)]

    qg = jnp.stack([queries, grad_out]).reshape(2, HEAD_DIM, CHIPS, -1).transpose(2, 0, 1, 3)
    chip_groups = [[CS * chip + core for chip in range(CHIPS)] for core in range(CS)]
    qg = lax.all_to_all(
        qg, "mp", split_axis=0, concat_axis=0, tiled=True, axis_index_groups=chip_groups
    )

    xor = lax.dynamic_index_in_dim(shard_blk, my_mp, 0, keepdims=False) ^ my_mp
    slots = lax.dynamic_index_in_dim(slot_blk, my_mp, 0, keepdims=False)
    where = jnp.stack([xor, slots], axis=1).reshape(dp_count, -1)
    where = jnp.stack([where[my_dp], where[1 - my_dp]]).reshape(-1).astype(jnp.int32)
    own, give = choose(where, near_pieces + far_pieces)
    got = swap_dp(give)
    span_shape = (CH_DEV, NBR * slice_len, E)
    own, got = own.reshape(span_shape), got.reshape(span_shape)
    neighbours = (own, got, swap(own, 1), swap(got, 1))

    result = attend(place, neighbours, (k0, kx, ky, kd, v0, vx, vy, vd), qg)
    back = lax.all_to_all(
        result, "mp", split_axis=0, concat_axis=0, tiled=True, axis_index_groups=chip_groups
    )
    back = back.transpose(1, 2, 0, 3).reshape((2,) + queries.shape)
    return back[0], back[1]


def general(queries, cache, cache_scale, w_kv, nbr_shard, nbr_row, grad_out):
    dp_count = lax.axis_size("dp")
    mp_count = lax.axis_size("mp")
    my_mp = lax.axis_index("mp")
    slice_len = cache.shape[1]
    most_slots = 2 * ((dp_count * CH_DEV * NBR + mp_count - 1) // mp_count)
    local_query = lax.all_to_all(queries, "mp", split_axis=1, concat_axis=0, tiled=True)
    shard_blk, row_blk, slot_blk = requests(nbr_shard, nbr_row, dp_count, mp_count)
    to_me = shard_blk == my_mp
    slot_ids = jnp.arange(most_slots, dtype=jnp.int32)
    select = jnp.logical_and(to_me[:, None, :], slot_blk[:, None, :] == slot_ids[None, :, None])
    wanted = jnp.sum(jnp.where(select, row_blk[:, None, :], 0), axis=2)
    sending = (cache[wanted].astype(jnp.float32) * cache_scale[wanted][..., None]).astype(
        jnp.bfloat16
    )
    arrived = lax.all_to_all(sending, "mp", split_axis=0, concat_axis=0, tiled=True)
    flat_pieces = arrived.reshape(mp_count * most_slots, slice_len, E)
    own_shards = lax.dynamic_index_in_dim(shard_blk, my_mp, 0, keepdims=False)
    own_slots = lax.dynamic_index_in_dim(slot_blk, my_mp, 0, keepdims=False)
    pieces = jnp.take(flat_pieces, own_shards * most_slots + own_slots, axis=0)
    pieces = pieces.reshape(dp_count, CH_DEV * NBR, slice_len, E)
    gathered = lax.all_to_all(pieces, "dp", split_axis=0, concat_axis=2, tiled=True)
    neighbours = gathered.reshape(CH_DEV, NBR * NT, E)
    gathered_weights = lax.all_gather(w_kv, ("dp", "mp"), axis=0, tiled=False)
    all_weights = (
        gathered_weights.reshape((dp_count, mp_count) + w_kv.shape)
        .transpose(2, 1, 3, 0, 4)
        .reshape(2, E, HEADS * HEAD_DIM)
    )
    key_value = jnp.einsum(
        "cte,ken->kctn", neighbours, all_weights, preferred_element_type=jnp.float32
    ).astype(jnp.bfloat16)
    key_rows = key_value[0].reshape(CH_DEV, NBR * NT, HEADS, HEAD_DIM)
    values = key_value[1].reshape(CH_DEV, NBR * NT, HEADS, HEAD_DIM)
    query_c = local_query.reshape(HEADS, HEAD_DIM, CH_DEV, SPAN)
    affinity_logits = (
        jnp.einsum("hdcq,ckhd->chqk", query_c, key_rows, preferred_element_type=jnp.float32)
        * SCORE_SCALE
    )
    row_max = jnp.max(affinity_logits, axis=3, keepdims=True)
    exponent = jnp.exp(affinity_logits - row_max)
    attn_probs = exponent / jnp.sum(exponent, axis=3, keepdims=True)
    probs_low = attn_probs.astype(jnp.bfloat16)
    output_c = jnp.einsum(
        "chqk,ckhd->hdcq", probs_low, values, preferred_element_type=jnp.float32
    ).astype(jnp.bfloat16)
    output_rows = output_c.reshape(HEADS * HEAD_DIM, CH_DEV * SPAN)
    output_back = lax.all_to_all(output_rows, "mp", split_axis=0, concat_axis=1, tiled=True)
    local_grad = lax.all_to_all(grad_out, "mp", split_axis=1, concat_axis=0, tiled=True)
    grad_c = local_grad.reshape(HEADS, HEAD_DIM, CH_DEV, SPAN)
    dprobs = jnp.einsum("hdcq,ckhd->chqk", grad_c, values, preferred_element_type=jnp.float32)
    row_delta = jnp.einsum("hdcq,hdcq->chq", grad_c, output_c, preferred_element_type=jnp.float32)
    dscores = (attn_probs * (dprobs - row_delta[..., None]) * SCORE_SCALE).astype(jnp.bfloat16)
    grad_query = jnp.einsum(
        "chqk,ckhd->hdcq", dscores, key_rows, preferred_element_type=jnp.float32
    ).astype(jnp.bfloat16)
    grad_rows = grad_query.reshape(HEADS * HEAD_DIM, CH_DEV * SPAN)
    grad_back = lax.all_to_all(grad_rows, "mp", split_axis=0, concat_axis=1, tiled=True)
    return (output_back, grad_back)


def solution(mesh):
    fits = mesh.shape["dp"] == 2 and mesh.shape["mp"] == len(ALL)
    return jax.shard_map(
        small if fits else general,
        mesh=mesh,
        in_specs=(
            P("mp", "dp"),
            P("mp", "dp", None),
            P("mp", "dp"),
            P(None, "mp", "dp"),
            P(),
            P(),
            P("mp", "dp"),
        ),
        out_specs=(P("mp", "dp"), P("mp", "dp")),
        check_vma=False,
    )
```

```python
import jax
import jax.numpy as jnp
from jax import lax
from jax.experimental import pallas as pl
from jax.experimental.pallas import tpu as pltpu
from jax.sharding import PartitionSpec as P

HEADS = 16
HEAD_DIM = 128
E = 896
NT = 128
SPAN = 64
NBR = 2
CH_DEV = 2
MOST = 2

SCORE_SCALE = HEAD_DIM ** (-0.5)


def requests(nbr_shard, nbr_row, dp_count, mp_count):
    block_size = dp_count * CH_DEV * NBR
    shard_blk = (
        nbr_shard.reshape(dp_count, mp_count, CH_DEV * NBR)
        .transpose(1, 0, 2)
        .reshape(mp_count, block_size)
    )
    row_blk = (
        nbr_row.reshape(dp_count, mp_count, CH_DEV * NBR)
        .transpose(1, 0, 2)
        .reshape(mp_count, block_size)
    )
    positions = jnp.arange(block_size, dtype=jnp.int32)
    earlier = positions[None, :] < positions[:, None]
    same_shard = shard_blk[:, :, None] == shard_blk[:, None, :]
    slot_blk = jnp.sum(jnp.logical_and(same_shard, earlier[None]), axis=2)
    return shard_blk, row_blk, slot_blk


ZS, XS, CS = 4, 2, 2
CHIPS = ZS * XS
HALF = 8
ALL = range(ZS * XS * CS)


def rows_kernel(rows_ref, src_ref, *outs):
    for k in range(HALF):
        for m in range(MOST):
            outs[k][m] = src_ref[rows_ref[k * MOST + m]]


def pick_rows(rows, source):
    piece = jax.ShapeDtypeStruct((MOST,) + source.shape[1:], source.dtype)
    return pl.pallas_call(
        rows_kernel,
        in_specs=[
            pl.BlockSpec(memory_space=pltpu.SMEM),
            pl.BlockSpec(memory_space=pltpu.VMEM),
        ],
        out_specs=[pl.BlockSpec(memory_space=pltpu.VMEM)] * HALF,
        out_shape=[piece] * HALF,
        compiler_params=pltpu.CompilerParams(vmem_limit_bytes=32 * 1024 * 1024),
        name="pick_rows",
    )(rows, source)


def choose_kernel(where_ref, *refs):
    count = 2 * HALF
    pieces, outs, sem = refs[:count], refs[count:-1], refs[-1]
    for r in range(2 * CH_DEV * NBR):
        out = outs[r // (CH_DEV * NBR)].at[r % (CH_DEV * NBR)]
        piece, slot = where_ref[2 * r], where_ref[2 * r + 1]
        for p in range(count):

            @pl.when(piece == p)
            def _():
                pltpu.make_async_copy(pieces[p].at[slot], out, sem.at[r]).start()

    for r in range(2 * CH_DEV * NBR):
        out = outs[r // (CH_DEV * NBR)].at[r % (CH_DEV * NBR)]
        pltpu.make_async_copy(pieces[0].at[0], out, sem.at[r]).wait()


def choose(where, pieces):
    half = jax.ShapeDtypeStruct((CH_DEV * NBR,) + pieces[0].shape[1:], pieces[0].dtype)
    return pl.pallas_call(
        choose_kernel,
        in_specs=[pl.BlockSpec(memory_space=pltpu.SMEM)]
        + [pl.BlockSpec(memory_space=pl.ANY)] * len(pieces),
        out_specs=[pl.BlockSpec(memory_space=pltpu.VMEM)] * 2,
        out_shape=[half] * 2,
        scratch_shapes=[pltpu.SemaphoreType.DMA((2 * CH_DEV * NBR,))],
        name="choose",
    )(where, *pieces)


def tdot(a, b):
    return lax.dot_general(a, b, (((0,), (0,)), ((), ())), preferred_element_type=jnp.float32)


def ndot(a, b):
    return jnp.dot(a, b, preferred_element_type=jnp.float32)


def attend_kernel(
    place_ref, na, nb, sa, sb, k0, kx, ky, kd, v0, vx, vy, vd, qg_ref, out_ref, n_scr, w_scr
):
    step = pl.program_id(0)
    d_heads = HEADS // CS // 2
    my_c, my_z, my_x = place_ref[1], place_ref[2], place_ref[3]
    rows = w_scr.shape[0] // CHIPS

    @pl.when(step == 0)
    def _():
        for s in range(CH_DEV):
            for core, first, second in ((my_c, na, nb), (1 - my_c, sa, sb)):
                n_scr[CH_DEV * core + s, 0:NT, :] = first[s]
                n_scr[CH_DEV * core + s, NT : 2 * NT, :] = second[s]

    def put(own, other, lane):
        for r in range(ZS):
            src_z = lax.rem(my_z - r + ZS, ZS)
            for x_at, ref in ((my_x, own), (1 - my_x, other)):
                at = pl.multiple_of((src_z * XS + x_at) * rows, 16)
                w_scr[pl.ds(at, rows), lane : lane + HEAD_DIM] = ref[r]

    @pl.when(step < d_heads)
    def _():
        put(k0, kx, 0)
        put(v0, vx, HEAD_DIM)

    @pl.when(step >= d_heads)
    def _():
        put(ky, kd, 0)
        put(vy, vd, HEAD_DIM)

    keys = NBR * NT
    weights = w_scr[...]
    lane = lax.broadcasted_iota(jnp.int32, (1, 2 * SPAN), 1)
    low = lane < SPAN
    for p in range(CS):
        kv = [
            ndot(n_scr[CH_DEV * p + s], weights).astype(jnp.bfloat16) for s in range(CH_DEV)
        ]
        ka, kb = kv[0][:, :HEAD_DIM], kv[1][:, :HEAD_DIM]
        va, vb = kv[0][:, HEAD_DIM:], kv[1][:, HEAD_DIM:]
        at = slice(2 * SPAN * p, 2 * SPAN * (p + 1))
        q = qg_ref[0, 0, :, at]
        g = qg_ref[0, 1, :, at]
        scores = jnp.where(low, ndot(ka, q), ndot(kb, q)) * SCORE_SCALE
        exponent = jnp.exp(scores - jnp.max(scores, axis=0, keepdims=True))
        probs = exponent / jnp.sum(exponent, axis=0, keepdims=True)
        probs_low = probs.astype(jnp.bfloat16)
        out = jnp.where(low, tdot(va, probs_low), tdot(vb, probs_low)).astype(jnp.bfloat16)
        dprobs = jnp.where(low, ndot(va, g), ndot(vb, g))
        delta = jnp.sum(
            g.astype(jnp.float32) * out.astype(jnp.float32), axis=0, keepdims=True
        )
        dscores = (probs * (dprobs - delta) * SCORE_SCALE).astype(jnp.bfloat16)
        dq = jnp.where(low, tdot(ka, dscores), tdot(kb, dscores)).astype(jnp.bfloat16)
        out_ref[0, 0, :, at] = out
        out_ref[0, 1, :, at] = dq


def attend(place, neighbours, weights, qg):
    d_heads = HEADS // CS // 2
    heads = 2 * d_heads
    tokens = qg.shape[-1]

    def whole(a):
        return pl.BlockSpec(a.shape, lambda i, place: (0,) * a.ndim)

    def own(a):
        return pl.BlockSpec(
            a.shape[:2] + (HEAD_DIM,), lambda i, place: (0, 0, jnp.minimum(i, d_heads - 1))
        )

    def other(a):
        return pl.BlockSpec(
            a.shape[:2] + (HEAD_DIM,), lambda i, place: (0, 0, jnp.maximum(i - d_heads, 0))
        )

    head_block = pl.BlockSpec(
        (1, 2, HEAD_DIM, tokens),
        lambda i, place: (lax.rem(i + d_heads * place[0], heads), 0, 0, 0),
    )
    return pl.pallas_call(
        attend_kernel,
        grid_spec=pltpu.PrefetchScalarGridSpec(
            num_scalar_prefetch=1,
            grid=(heads,),
            in_specs=[whole(a) for a in neighbours]
            + [f(a) for f, a in zip((own, own, other, other) * 2, weights)]
            + [head_block],
            out_specs=head_block,
            scratch_shapes=[
                pltpu.VMEM((CS * CH_DEV, NBR * NT, E), jnp.bfloat16),
                pltpu.VMEM((E, 2 * HEAD_DIM), jnp.bfloat16),
            ],
        ),
        out_shape=jax.ShapeDtypeStruct(qg.shape, jnp.bfloat16),
        compiler_params=pltpu.CompilerParams(vmem_limit_bytes=40 * 1024 * 1024),
        name="attend",
    )(place, *neighbours, *weights, qg)


def small(queries, cache, cache_scale, w_kv, nbr_shard, nbr_row, grad_out):
    dp_count = lax.axis_size("dp")
    mp_count = lax.axis_size("mp")
    my_dp = lax.axis_index("dp")
    my_mp = lax.axis_index("mp")
    my_c, my_x, my_z = my_mp & 1, (my_mp >> 1) & 1, my_mp >> 2
    place = jnp.stack([my_dp, my_c, my_z, my_x]).astype(jnp.int32)
    slice_len = cache.shape[1]
    e_loc = w_kv.shape[1]

    def swap(a, bits):
        return lax.ppermute(a, "mp", [(m, m ^ bits) for m in ALL])

    def swap_dp(a):
        return lax.ppermute(a, "dp", [(0, 1), (1, 0)])

    by_parity = w_kv.reshape(2, e_loc, -1, CS, HEAD_DIM)
    mine = lax.dynamic_index_in_dim(by_parity, my_c, 3, keepdims=False).reshape(2, e_loc, -1)
    sends = lax.dynamic_index_in_dim(by_parity, 1 - my_c, 3, keepdims=False).reshape(2, e_loc, -1)
    came = swap(sends, 1)
    first = my_c == 0
    chip_w = jnp.concatenate(
        [jnp.where(first, mine, came), jnp.where(first, came, mine)], axis=1
    )

    scaled = (cache.astype(jnp.float32) * cache_scale[..., None]).astype(jnp.bfloat16)
    far = swap(scaled, HALF)
    shard_blk, row_blk, slot_blk = requests(nbr_shard, nbr_row, dp_count, mp_count)
    holders = jnp.stack([my_mp, my_mp ^ HALF]).astype(jnp.int32)
    takers = my_mp ^ jnp.arange(HALF, dtype=jnp.int32)
    select = jnp.logical_and(
        shard_blk[:, None, None, :] == holders[None, :, None, None],
        slot_blk[:, None, None, :] == jnp.arange(MOST, dtype=jnp.int32)[None, None, :, None],
    )
    wanted = jnp.sum(jnp.where(select, row_blk[:, None, None, :], 0), axis=3)[takers]
    near_pieces = pick_rows(wanted[:, 0].reshape(-1), scaled)
    near_pieces = [near_pieces[0]] + [swap(near_pieces[k], k) for k in range(1, HALF)]

    turned = [chip_w] + [
        lax.ppermute(chip_w, "mp", [(m, (m + XS * CS * r) % len(ALL)) for m in ALL])
        for r in range(1, ZS)
    ]
    k0 = jnp.stack([t[0] for t in turned])
    v0 = jnp.stack([t[1] for t in turned])
    kx, vy = swap(k0, CS), swap_dp(v0)
    vx, ky = swap(v0, CS), swap_dp(k0)
    vd, kd = swap(vy, CS), swap_dp(kx)

    far_pieces = pick_rows(wanted[:, 1].reshape(-1), far)
    far_pieces = [far_pieces[0]] + [swap(far_pieces[k], k) for k in range(1, HALF)]

    qg = jnp.stack([queries, grad_out]).reshape(2, HEAD_DIM, CHIPS, -1).transpose(2, 0, 1, 3)
    chip_groups = [[CS * chip + core for chip in range(CHIPS)] for core in range(CS)]
    qg = lax.all_to_all(
        qg, "mp", split_axis=0, concat_axis=0, tiled=True, axis_index_groups=chip_groups
    )

    xor = lax.dynamic_index_in_dim(shard_blk, my_mp, 0, keepdims=False) ^ my_mp
    slots = lax.dynamic_index_in_dim(slot_blk, my_mp, 0, keepdims=False)
    where = jnp.stack([xor, slots], axis=1).reshape(dp_count, -1)
    where = jnp.stack([where[my_dp], where[1 - my_dp]]).reshape(-1).astype(jnp.int32)
    own, give = choose(where, near_pieces + far_pieces)
    got = swap_dp(give)
    span_shape = (CH_DEV, NBR * slice_len, E)
    own, got = own.reshape(span_shape), got.reshape(span_shape)
    neighbours = (own, got, swap(own, 1), swap(got, 1))

    result = attend(place, neighbours, (k0, kx, ky, kd, v0, vx, vy, vd), qg)
    back = lax.all_to_all(
        result, "mp", split_axis=0, concat_axis=0, tiled=True, axis_index_groups=chip_groups
    )
    back = back.transpose(1, 2, 0, 3).reshape((2,) + queries.shape)
    return back[0], back[1]


def general(queries, cache, cache_scale, w_kv, nbr_shard, nbr_row, grad_out):
    dp_count = lax.axis_size("dp")
    mp_count = lax.axis_size("mp")
    my_mp = lax.axis_index("mp")
    slice_len = cache.shape[1]
    most_slots = 2 * ((dp_count * CH_DEV * NBR + mp_count - 1) // mp_count)
    local_query = lax.all_to_all(queries, "mp", split_axis=1, concat_axis=0, tiled=True)
    shard_blk, row_blk, slot_blk = requests(nbr_shard, nbr_row, dp_count, mp_count)
    to_me = shard_blk == my_mp
    slot_ids = jnp.arange(most_slots, dtype=jnp.int32)
    select = jnp.logical_and(to_me[:, None, :], slot_blk[:, None, :] == slot_ids[None, :, None])
    wanted = jnp.sum(jnp.where(select, row_blk[:, None, :], 0), axis=2)
    sending = (cache[wanted].astype(jnp.float32) * cache_scale[wanted][..., None]).astype(
        jnp.bfloat16
    )
    arrived = lax.all_to_all(sending, "mp", split_axis=0, concat_axis=0, tiled=True)
    flat_pieces = arrived.reshape(mp_count * most_slots, slice_len, E)
    own_shards = lax.dynamic_index_in_dim(shard_blk, my_mp, 0, keepdims=False)
    own_slots = lax.dynamic_index_in_dim(slot_blk, my_mp, 0, keepdims=False)
    pieces = jnp.take(flat_pieces, own_shards * most_slots + own_slots, axis=0)
    pieces = pieces.reshape(dp_count, CH_DEV * NBR, slice_len, E)
    gathered = lax.all_to_all(pieces, "dp", split_axis=0, concat_axis=2, tiled=True)
    neighbours = gathered.reshape(CH_DEV, NBR * NT, E)
    gathered_weights = lax.all_gather(w_kv, ("dp", "mp"), axis=0, tiled=False)
    all_weights = (
        gathered_weights.reshape((dp_count, mp_count) + w_kv.shape)
        .transpose(2, 1, 3, 0, 4)
        .reshape(2, E, HEADS * HEAD_DIM)
    )
    key_value = jnp.einsum(
        "cte,ken->kctn", neighbours, all_weights, preferred_element_type=jnp.float32
    ).astype(jnp.bfloat16)
    key_rows = key_value[0].reshape(CH_DEV, NBR * NT, HEADS, HEAD_DIM)
    values = key_value[1].reshape(CH_DEV, NBR * NT, HEADS, HEAD_DIM)
    query_c = local_query.reshape(HEADS, HEAD_DIM, CH_DEV, SPAN)
    affinity_logits = (
        jnp.einsum("hdcq,ckhd->chqk", query_c, key_rows, preferred_element_type=jnp.float32)
        * SCORE_SCALE
    )
    row_max = jnp.max(affinity_logits, axis=3, keepdims=True)
    exponent = jnp.exp(affinity_logits - row_max)
    attn_probs = exponent / jnp.sum(exponent, axis=3, keepdims=True)
    probs_low = attn_probs.astype(jnp.bfloat16)
    output_c = jnp.einsum(
        "chqk,ckhd->hdcq", probs_low, values, preferred_element_type=jnp.float32
    ).astype(jnp.bfloat16)
    output_rows = output_c.reshape(HEADS * HEAD_DIM, CH_DEV * SPAN)
    output_back = lax.all_to_all(output_rows, "mp", split_axis=0, concat_axis=1, tiled=True)
    local_grad = lax.all_to_all(grad_out, "mp", split_axis=1, concat_axis=0, tiled=True)
    grad_c = local_grad.reshape(HEADS, HEAD_DIM, CH_DEV, SPAN)
    dprobs = jnp.einsum("hdcq,ckhd->chqk", grad_c, values, preferred_element_type=jnp.float32)
    row_delta = jnp.einsum("hdcq,hdcq->chq", grad_c, output_c, preferred_element_type=jnp.float32)
    dscores = (attn_probs * (dprobs - row_delta[..., None]) * SCORE_SCALE).astype(jnp.bfloat16)
    grad_query = jnp.einsum(
        "chqk,ckhd->hdcq", dscores, key_rows, preferred_element_type=jnp.float32
    ).astype(jnp.bfloat16)
    grad_rows = grad_query.reshape(HEADS * HEAD_DIM, CH_DEV * SPAN)
    grad_back = lax.all_to_all(grad_rows, "mp", split_axis=0, concat_axis=1, tiled=True)
    return (output_back, grad_back)


def solution(mesh):
    fits = mesh.shape["dp"] == 2 and mesh.shape["mp"] == len(ALL)
    return jax.shard_map(
        small if fits else general,
        mesh=mesh,
        in_specs=(
            P("mp", "dp"),
            P("mp", "dp", None),
            P("mp", "dp"),
            P(None, "mp", "dp"),
            P(),
            P(),
            P("mp", "dp"),
        ),
        out_specs=(P("mp", "dp"), P("mp", "dp")),
        check_vma=False,
    )
```

```python
import jax
import jax.numpy as jnp
from jax import lax
from jax.experimental import pallas as pl
from jax.experimental.pallas import tpu as pltpu
from jax.sharding import PartitionSpec as P

HEADS = 16
HEAD_DIM = 128
E = 896
NT = 128
SPAN = 64
NBR = 2
CH_DEV = 2
MOST = 2

SCORE_SCALE = HEAD_DIM ** (-0.5)


def requests(nbr_shard, nbr_row, dp_count, mp_count):
    block_size = dp_count * CH_DEV * NBR
    shard_blk = (
        nbr_shard.reshape(dp_count, mp_count, CH_DEV * NBR)
        .transpose(1, 0, 2)
        .reshape(mp_count, block_size)
    )
    row_blk = (
        nbr_row.reshape(dp_count, mp_count, CH_DEV * NBR)
        .transpose(1, 0, 2)
        .reshape(mp_count, block_size)
    )
    positions = jnp.arange(block_size, dtype=jnp.int32)
    earlier = positions[None, :] < positions[:, None]
    same_shard = shard_blk[:, :, None] == shard_blk[:, None, :]
    slot_blk = jnp.sum(jnp.logical_and(same_shard, earlier[None]), axis=2)
    return shard_blk, row_blk, slot_blk


ZS, XS, CS = 4, 2, 2
CHIPS = ZS * XS
HALF = 8
ALL = range(ZS * XS * CS)


def parity_kernel(core_ref, w_ref, mine_ref, sends_ref):
    for core in range(CS):

        @pl.when(core_ref[0] == core)
        def _():
            for j in range(HEADS // CS // 2):
                at = slice(j * HEAD_DIM, (j + 1) * HEAD_DIM)
                for ref, parity in ((mine_ref, core), (sends_ref, 1 - core)):
                    head = CS * j + parity
                    ref[:, :, at] = w_ref[:, :, head * HEAD_DIM : (head + 1) * HEAD_DIM]


def by_parity(core, w_kv):
    half = jax.ShapeDtypeStruct(w_kv.shape[:2] + (w_kv.shape[2] // CS,), w_kv.dtype)
    return pl.pallas_call(
        parity_kernel,
        in_specs=[
            pl.BlockSpec(memory_space=pltpu.SMEM),
            pl.BlockSpec(memory_space=pltpu.VMEM),
        ],
        out_specs=[pl.BlockSpec(memory_space=pltpu.VMEM)] * 2,
        out_shape=[half] * 2,
        name="by_parity",
    )(core, w_kv)


def rows_kernel(rows_ref, src_ref, out_ref):
    for k in range(out_ref.shape[0]):
        out_ref[k] = src_ref[rows_ref[k]]


def pick_rows(rows, source):
    return pl.pallas_call(
        rows_kernel,
        in_specs=[
            pl.BlockSpec(memory_space=pltpu.SMEM),
            pl.BlockSpec(memory_space=pltpu.VMEM),
        ],
        out_specs=pl.BlockSpec(memory_space=pltpu.VMEM),
        out_shape=jax.ShapeDtypeStruct(rows.shape + source.shape[1:], source.dtype),
        compiler_params=pltpu.CompilerParams(vmem_limit_bytes=32 * 1024 * 1024),
        name="pick_rows",
    )(rows, source)


def choose_kernel(far_ref, row_ref, near, far, own, give, sem):
    each = CH_DEV * NBR
    outs = [(own if r < each else give).at[r % each] for r in range(2 * each)]
    for r, out in enumerate(outs):

        @pl.when(far_ref[r] == 0)
        def _():
            pltpu.make_async_copy(near.at[row_ref[r]], out, sem.at[r]).start()

        @pl.when(far_ref[r] != 0)
        def _():
            pltpu.make_async_copy(far.at[row_ref[r]], out, sem.at[r]).start()

    for r, out in enumerate(outs):
        pltpu.make_async_copy(near.at[0], out, sem.at[r]).wait()


def choose(is_far, row, near, far):
    half = jax.ShapeDtypeStruct((CH_DEV * NBR,) + near.shape[1:], near.dtype)
    return pl.pallas_call(
        choose_kernel,
        in_specs=[pl.BlockSpec(memory_space=pltpu.SMEM)] * 2
        + [pl.BlockSpec(memory_space=pl.ANY)] * 2,
        out_specs=[pl.BlockSpec(memory_space=pltpu.VMEM)] * 2,
        out_shape=[half] * 2,
        scratch_shapes=[pltpu.SemaphoreType.DMA((2 * CH_DEV * NBR,))],
        name="choose",
    )(is_far, row, near, far)


def tdot(a, b):
    return lax.dot_general(a, b, (((0,), (0,)), ((), ())), preferred_element_type=jnp.float32)


def ndot(a, b):
    return jnp.dot(a, b, preferred_element_type=jnp.float32)


def attend_kernel(
    place_ref, na, nb, sa, sb, w_own, w_x, w_y, w_xy, qg_ref, out_ref, n_scr, w_scr
):
    my_c, my_x, my_z = place_ref[1], place_ref[2], place_ref[3]
    rows = w_scr.shape[0] // CHIPS

    @pl.when(pl.program_id(0) == 0)
    def _():
        for s in range(CH_DEV):
            for core, first, second in ((my_c, na, nb), (1 - my_c, sa, sb)):
                n_scr[CH_DEV * core + s, 0:NT, :] = first[s]
                n_scr[CH_DEV * core + s, NT : 2 * NT, :] = second[s]

    def put(*sources):
        for r in range(ZS):
            src_z = lax.rem(my_z - r + ZS, ZS)
            for other, ref in enumerate(sources):
                at = pl.multiple_of((src_z * XS + (my_x ^ other)) * rows, 16)
                for kv in range(2):
                    lanes = slice(HEAD_DIM * kv, HEAD_DIM * (kv + 1))
                    w_scr[pl.ds(at, rows), lanes] = ref[r, kv]

    own_dp = pl.program_id(0) < pl.num_programs(0) // 2

    @pl.when(own_dp)
    def _():
        put(w_own, w_x)

    @pl.when(jnp.logical_not(own_dp))
    def _():
        put(w_y, w_xy)

    weights = w_scr[...]
    kvs = [ndot(n_scr[s], weights).astype(jnp.bfloat16) for s in range(CS * CH_DEV)]
    keys = [kv[:, :HEAD_DIM] for kv in kvs]
    values = [kv[:, HEAD_DIM:] for kv in kvs]
    low = lax.broadcasted_iota(jnp.int32, (1, 2 * SPAN), 1) < SPAN
    pairs = range(CS)
    lanes = [slice(2 * SPAN * p, 2 * SPAN * (p + 1)) for p in pairs]

    def both(dot, spans, right):
        return [
            jnp.where(low, dot(spans[2 * p], right[p]), dot(spans[2 * p + 1], right[p]))
            for p in pairs
        ]

    queries = [qg_ref[0, 0, :, at] for at in lanes]
    grads = [qg_ref[0, 1, :, at] for at in lanes]
    scores = [s * SCORE_SCALE for s in both(ndot, keys, queries)]
    dprobs = both(ndot, values, grads)
    exponent = [jnp.exp(s - jnp.max(s, axis=0, keepdims=True)) for s in scores]
    probs = [e * (1.0 / jnp.sum(e, axis=0, keepdims=True)) for e in exponent]
    probs_low = [p.astype(jnp.bfloat16) for p in probs]
    outs = [o.astype(jnp.bfloat16) for o in both(tdot, values, probs_low)]
    delta = [
        jnp.sum(g.astype(jnp.float32) * o.astype(jnp.float32), axis=0, keepdims=True)
        for g, o in zip(grads, outs)
    ]
    dscores = [
        (p * (dp - dl) * SCORE_SCALE).astype(jnp.bfloat16)
        for p, dp, dl in zip(probs, dprobs, delta)
    ]
    dqs = [q.astype(jnp.bfloat16) for q in both(tdot, keys, dscores)]
    for p in pairs:
        out_ref[0, 0, :, lanes[p]] = outs[p]
        out_ref[0, 1, :, lanes[p]] = dqs[p]


def attend(place, neighbours, weights, qg):
    d_heads = HEADS // CS // 2
    heads = 2 * d_heads
    block = (1, 2, HEAD_DIM, qg.shape[-1])

    def head_of(i, place):
        return (i + d_heads * place[0]) & (heads - 1)

    def came_at(i, place):
        head = head_of(i, place)
        half = head // d_heads
        return (2 * (head & (d_heads - 1)) + jnp.abs(half - place[3] // 2), 0, 0, 0)

    w_block = weights[0].shape[:3] + (HEAD_DIM,)
    first = pl.BlockSpec(w_block, lambda i, place: (0, 0, 0, jnp.minimum(i, d_heads - 1)))
    last = pl.BlockSpec(w_block, lambda i, place: (0, 0, 0, jnp.maximum(i - d_heads, 0)))
    return pl.pallas_call(
        attend_kernel,
        grid_spec=pltpu.PrefetchScalarGridSpec(
            num_scalar_prefetch=1,
            grid=(heads,),
            in_specs=[
                pl.BlockSpec(a.shape, lambda i, place: (0, 0, 0)) for a in neighbours
            ]
            + [first, first, last, last, pl.BlockSpec(block, came_at)],
            out_specs=pl.BlockSpec(block, lambda i, place: (head_of(i, place), 0, 0, 0)),
            scratch_shapes=[
                pltpu.VMEM((CS * CH_DEV, NBR * NT, E), jnp.bfloat16),
                pltpu.VMEM((E, 2 * HEAD_DIM), jnp.bfloat16),
            ],
        ),
        out_shape=jax.ShapeDtypeStruct(qg.shape, jnp.bfloat16),
        compiler_params=pltpu.CompilerParams(vmem_limit_bytes=40 * 1024 * 1024),
        name="attend",
    )(place, *neighbours, *weights, qg)


def small(queries, cache, cache_scale, w_kv, nbr_shard, nbr_row, grad_out):
    dp_count = lax.axis_size("dp")
    mp_count = lax.axis_size("mp")
    my_dp = lax.axis_index("dp")
    my_mp = lax.axis_index("mp")
    my_c, my_x, my_z = my_mp & 1, (my_mp >> 1) & 1, my_mp >> 2
    place = jnp.stack([my_dp, my_c, my_x, my_z]).astype(jnp.int32)
    slice_len = cache.shape[1]

    def swap(a, bits):
        return lax.ppermute(a, "mp", [(m, m ^ bits) for m in ALL])

    def swap_dp(a):
        return lax.ppermute(a, "dp", [(0, 1), (1, 0)])

    def over_half(a):
        halves = [list(range(HALF)), list(range(HALF, 2 * HALF))]
        return lax.all_to_all(
            a, "mp", split_axis=0, concat_axis=0, tiled=True, axis_index_groups=halves
        )

    turned = [w_kv] + [
        lax.ppermute(w_kv, "mp", [(m, (m + XS * CS * r) % len(ALL)) for m in ALL])
        for r in range(1, ZS)
    ]
    scaled = (cache.astype(jnp.float32) * cache_scale[..., None]).astype(jnp.bfloat16)
    scaled, turned = lax.optimization_barrier((scaled, turned))
    far = swap(scaled, HALF)

    mine, sends = by_parity(my_c.reshape(1).astype(jnp.int32), jnp.concatenate(turned))
    came = swap(sends, 1)
    line_w = jnp.where(
        my_c == 0,
        jnp.concatenate([mine, came], axis=1),
        jnp.concatenate([came, mine], axis=1),
    ).reshape(ZS, 2, CS * w_kv.shape[1], -1)
    x_w, y_w = swap(line_w, CS), swap_dp(line_w)

    shard_blk, row_blk, slot_blk = requests(nbr_shard, nbr_row, dp_count, mp_count)
    holders = jnp.stack([my_mp, my_mp ^ HALF]).astype(jnp.int32)
    select = jnp.logical_and(
        shard_blk[:, None, None, :] == holders[None, :, None, None],
        slot_blk[:, None, None, :] == jnp.arange(MOST, dtype=jnp.int32)[None, None, :, None],
    )
    wanted = jnp.sum(jnp.where(select, row_blk[:, None, None, :], 0), axis=3)
    wanted = lax.dynamic_slice_in_dim(wanted, my_mp & HALF, HALF, 0)

    def pieces(which, *sources):
        rows = pick_rows(wanted[:, which].reshape(-1), *sources)
        return over_half(rows.reshape((HALF, MOST) + rows.shape[1:])).reshape(rows.shape)

    near_source, line_w = lax.optimization_barrier((scaled, line_w))
    near_pieces = pieces(0, near_source)

    my_half = my_mp // HALF
    chips = CHIPS // 2
    qg = jnp.stack([queries, grad_out]).reshape(2, HEAD_DIM, CHIPS, -1).transpose(2, 0, 1, 3)
    qg = qg.reshape((2, chips) + qg.shape[1:])
    qg_stay = lax.dynamic_index_in_dim(qg, my_half, 0, keepdims=False)
    qg_go = lax.dynamic_index_in_dim(qg, 1 - my_half, 0, keepdims=False)

    far, near_pieces, x_w, y_w, qg_go = lax.optimization_barrier(
        (far, near_pieces, x_w, y_w, qg_go)
    )
    xy_w = swap_dp(x_w)
    far_pieces = pieces(1, far)
    qg_came = swap(qg_go, HALF)

    far_pieces, qg_came, xy_w = lax.optimization_barrier((far_pieces, qg_came, xy_w))
    chip_lines = [
        [HALF * half + CS * chip + core for chip in range(chips)]
        for half in range(2)
        for core in range(CS)
    ]
    qg = lax.all_to_all(
        jnp.stack([qg_stay, qg_came], axis=1),
        "mp",
        split_axis=0,
        concat_axis=0,
        tiled=True,
        axis_index_groups=chip_lines,
    )
    qg = qg.reshape((CHIPS,) + qg.shape[2:])
    chip_groups = [[CS * chip + core for chip in range(CHIPS)] for core in range(CS)]

    shards = lax.dynamic_index_in_dim(shard_blk, my_mp, 0, keepdims=False)
    slots = lax.dynamic_index_in_dim(slot_blk, my_mp, 0, keepdims=False)
    row = jnp.roll(((shards & (HALF - 1)) * MOST + slots).reshape(dp_count, -1), my_dp, 0)
    is_far = jnp.roll(((shards ^ my_mp) & HALF).reshape(dp_count, -1), my_dp, 0)
    own, give = choose(
        is_far.reshape(-1).astype(jnp.int32),
        row.reshape(-1).astype(jnp.int32),
        near_pieces,
        far_pieces,
    )
    got = swap_dp(give)
    span_shape = (CH_DEV, NBR * slice_len, E)
    own, got = own.reshape(span_shape), got.reshape(span_shape)
    neighbours = (own, got, swap(own, 1), swap(got, 1))

    result = attend(place, neighbours, (line_w, x_w, y_w, xy_w), qg)
    back = lax.all_to_all(
        result, "mp", split_axis=0, concat_axis=0, tiled=True, axis_index_groups=chip_groups
    )
    back = back.transpose(1, 2, 0, 3).reshape((2,) + queries.shape)
    return back[0], back[1]


def general(queries, cache, cache_scale, w_kv, nbr_shard, nbr_row, grad_out):
    dp_count = lax.axis_size("dp")
    mp_count = lax.axis_size("mp")
    my_mp = lax.axis_index("mp")
    slice_len = cache.shape[1]
    most_slots = 2 * ((dp_count * CH_DEV * NBR + mp_count - 1) // mp_count)
    local_query = lax.all_to_all(queries, "mp", split_axis=1, concat_axis=0, tiled=True)
    shard_blk, row_blk, slot_blk = requests(nbr_shard, nbr_row, dp_count, mp_count)
    to_me = shard_blk == my_mp
    slot_ids = jnp.arange(most_slots, dtype=jnp.int32)
    select = jnp.logical_and(to_me[:, None, :], slot_blk[:, None, :] == slot_ids[None, :, None])
    wanted = jnp.sum(jnp.where(select, row_blk[:, None, :], 0), axis=2)
    sending = (cache[wanted].astype(jnp.float32) * cache_scale[wanted][..., None]).astype(
        jnp.bfloat16
    )
    arrived = lax.all_to_all(sending, "mp", split_axis=0, concat_axis=0, tiled=True)
    flat_pieces = arrived.reshape(mp_count * most_slots, slice_len, E)
    own_shards = lax.dynamic_index_in_dim(shard_blk, my_mp, 0, keepdims=False)
    own_slots = lax.dynamic_index_in_dim(slot_blk, my_mp, 0, keepdims=False)
    pieces = jnp.take(flat_pieces, own_shards * most_slots + own_slots, axis=0)
    pieces = pieces.reshape(dp_count, CH_DEV * NBR, slice_len, E)
    gathered = lax.all_to_all(pieces, "dp", split_axis=0, concat_axis=2, tiled=True)
    neighbours = gathered.reshape(CH_DEV, NBR * NT, E)
    gathered_weights = lax.all_gather(w_kv, ("dp", "mp"), axis=0, tiled=False)
    all_weights = (
        gathered_weights.reshape((dp_count, mp_count) + w_kv.shape)
        .transpose(2, 1, 3, 0, 4)
        .reshape(2, E, HEADS * HEAD_DIM)
    )
    key_value = jnp.einsum(
        "cte,ken->kctn", neighbours, all_weights, preferred_element_type=jnp.float32
    ).astype(jnp.bfloat16)
    key_rows = key_value[0].reshape(CH_DEV, NBR * NT, HEADS, HEAD_DIM)
    values = key_value[1].reshape(CH_DEV, NBR * NT, HEADS, HEAD_DIM)
    query_c = local_query.reshape(HEADS, HEAD_DIM, CH_DEV, SPAN)
    affinity_logits = (
        jnp.einsum("hdcq,ckhd->chqk", query_c, key_rows, preferred_element_type=jnp.float32)
        * SCORE_SCALE
    )
    row_max = jnp.max(affinity_logits, axis=3, keepdims=True)
    exponent = jnp.exp(affinity_logits - row_max)
    attn_probs = exponent / jnp.sum(exponent, axis=3, keepdims=True)
    probs_low = attn_probs.astype(jnp.bfloat16)
    output_c = jnp.einsum(
        "chqk,ckhd->hdcq", probs_low, values, preferred_element_type=jnp.float32
    ).astype(jnp.bfloat16)
    output_rows = output_c.reshape(HEADS * HEAD_DIM, CH_DEV * SPAN)
    output_back = lax.all_to_all(output_rows, "mp", split_axis=0, concat_axis=1, tiled=True)
    local_grad = lax.all_to_all(grad_out, "mp", split_axis=1, concat_axis=0, tiled=True)
    grad_c = local_grad.reshape(HEADS, HEAD_DIM, CH_DEV, SPAN)
    dprobs = jnp.einsum("hdcq,ckhd->chqk", grad_c, values, preferred_element_type=jnp.float32)
    row_delta = jnp.einsum("hdcq,hdcq->chq", grad_c, output_c, preferred_element_type=jnp.float32)
    dscores = (attn_probs * (dprobs - row_delta[..., None]) * SCORE_SCALE).astype(jnp.bfloat16)
    grad_query = jnp.einsum(
        "chqk,ckhd->hdcq", dscores, key_rows, preferred_element_type=jnp.float32
    ).astype(jnp.bfloat16)
    grad_rows = grad_query.reshape(HEADS * HEAD_DIM, CH_DEV * SPAN)
    grad_back = lax.all_to_all(grad_rows, "mp", split_axis=0, concat_axis=1, tiled=True)
    return (output_back, grad_back)


def solution(mesh):
    fits = mesh.shape["dp"] == 2 and mesh.shape["mp"] == len(ALL)
    return jax.shard_map(
        small if fits else general,
        mesh=mesh,
        in_specs=(
            P("mp", "dp"),
            P("mp", "dp", None),
            P("mp", "dp"),
            P(None, "mp", "dp"),
            P(),
            P(),
            P("mp", "dp"),
        ),
        out_specs=(P("mp", "dp"), P("mp", "dp")),
        check_vma=False,
    )
```

```python
import jax
import jax.numpy as jnp
from jax import lax
from jax.experimental import pallas as pl
from jax.experimental.pallas import tpu as pltpu
from jax.sharding import PartitionSpec as P

HEADS = 16
HEAD_DIM = 128
E = 896
NT = 128
SPAN = 64
NBR = 2
CH_DEV = 2
MOST = 2

SCORE_SCALE = HEAD_DIM ** (-0.5)


def requests(nbr_shard, nbr_row, dp_count, mp_count):
    block_size = dp_count * CH_DEV * NBR
    shard_blk = (
        nbr_shard.reshape(dp_count, mp_count, CH_DEV * NBR)
        .transpose(1, 0, 2)
        .reshape(mp_count, block_size)
    )
    row_blk = (
        nbr_row.reshape(dp_count, mp_count, CH_DEV * NBR)
        .transpose(1, 0, 2)
        .reshape(mp_count, block_size)
    )
    positions = jnp.arange(block_size, dtype=jnp.int32)
    earlier = positions[None, :] < positions[:, None]
    same_shard = shard_blk[:, :, None] == shard_blk[:, None, :]
    slot_blk = jnp.sum(jnp.logical_and(same_shard, earlier[None]), axis=2)
    return shard_blk, row_blk, slot_blk


ZS, XS, CS = 4, 2, 2
CHIPS = ZS * XS
HALF = 8
PER_STEP = 2
ALL = range(ZS * XS * CS)


def parity_kernel(core_ref, w_ref, mine_ref, sends_ref):
    for core in range(CS):

        @pl.when(core_ref[0] == core)
        def _():
            for j in range(HEADS // CS // 2):
                at = slice(j * HEAD_DIM, (j + 1) * HEAD_DIM)
                for ref, parity in ((mine_ref, core), (sends_ref, 1 - core)):
                    head = CS * j + parity
                    ref[:, :, at] = w_ref[:, :, head * HEAD_DIM : (head + 1) * HEAD_DIM]


def by_parity(core, w_kv):
    half = jax.ShapeDtypeStruct(w_kv.shape[:2] + (w_kv.shape[2] // CS,), w_kv.dtype)
    return pl.pallas_call(
        parity_kernel,
        in_specs=[
            pl.BlockSpec(memory_space=pltpu.SMEM),
            pl.BlockSpec(memory_space=pltpu.VMEM),
        ],
        out_specs=[pl.BlockSpec(memory_space=pltpu.VMEM)] * 2,
        out_shape=[half] * 2,
        name="by_parity",
    )(core, w_kv)


def rows_kernel(rows_ref, src_ref, out_ref):
    for k in range(out_ref.shape[0]):
        out_ref[k] = src_ref[rows_ref[k]]


def pick_rows(rows, source):
    return pl.pallas_call(
        rows_kernel,
        in_specs=[
            pl.BlockSpec(memory_space=pltpu.SMEM),
            pl.BlockSpec(memory_space=pltpu.VMEM),
        ],
        out_specs=pl.BlockSpec(memory_space=pltpu.VMEM),
        out_shape=jax.ShapeDtypeStruct(rows.shape + source.shape[1:], source.dtype),
        compiler_params=pltpu.CompilerParams(vmem_limit_bytes=32 * 1024 * 1024),
        name="pick_rows",
    )(rows, source)


def choose_kernel(far_ref, row_ref, near, far, own, give, sem):
    each = CH_DEV * NBR
    outs = [(own if r < each else give).at[r % each] for r in range(2 * each)]
    for r, out in enumerate(outs):

        @pl.when(far_ref[r] == 0)
        def _():
            pltpu.make_async_copy(near.at[row_ref[r]], out, sem.at[r]).start()

        @pl.when(far_ref[r] != 0)
        def _():
            pltpu.make_async_copy(far.at[row_ref[r]], out, sem.at[r]).start()

    for r, out in enumerate(outs):
        pltpu.make_async_copy(near.at[0], out, sem.at[r]).wait()


def choose(is_far, row, near, far):
    half = jax.ShapeDtypeStruct((CH_DEV * NBR,) + near.shape[1:], near.dtype)
    return pl.pallas_call(
        choose_kernel,
        in_specs=[pl.BlockSpec(memory_space=pltpu.SMEM)] * 2
        + [pl.BlockSpec(memory_space=pl.ANY)] * 2,
        out_specs=[pl.BlockSpec(memory_space=pltpu.VMEM)] * 2,
        out_shape=[half] * 2,
        scratch_shapes=[pltpu.SemaphoreType.DMA((2 * CH_DEV * NBR,))],
        name="choose",
    )(is_far, row, near, far)


def tdot(a, b):
    return lax.dot_general(a, b, (((0,), (0,)), ((), ())), preferred_element_type=jnp.float32)


def ndot(a, b):
    return jnp.dot(a, b, preferred_element_type=jnp.float32)


def attend_kernel(
    place_ref, na, nb, sa, sb, w_own, w_x, w_y, w_xy, qg_ref, out_ref, n_scr, w_scr
):
    my_c, my_x, my_z = place_ref[1], place_ref[2], place_ref[3]
    rows, width = w_scr.shape[0] // CHIPS, w_scr.shape[1] // 2

    @pl.when(pl.program_id(0) == 0)
    def _():
        for s in range(CH_DEV):
            for core, first, second in ((my_c, na, nb), (1 - my_c, sa, sb)):
                n_scr[CH_DEV * core + s, 0:NT, :] = first[s]
                n_scr[CH_DEV * core + s, NT : 2 * NT, :] = second[s]

    def put(*sources):
        for r in range(ZS):
            src_z = lax.rem(my_z - r + ZS, ZS)
            for other, ref in enumerate(sources):
                at = pl.multiple_of((src_z * XS + (my_x ^ other)) * rows, 16)
                for kv in range(2):
                    lanes = slice(width * kv, width * (kv + 1))
                    w_scr[pl.ds(at, rows), lanes] = ref[r, kv]

    own_dp = pl.program_id(0) < pl.num_programs(0) // 2

    @pl.when(own_dp)
    def _():
        put(w_own, w_x)

    @pl.when(jnp.logical_not(own_dp))
    def _():
        put(w_y, w_xy)

    weights = w_scr[...]
    kvs = [ndot(n_scr[s], weights).astype(jnp.bfloat16) for s in range(CS * CH_DEV)]
    low = lax.broadcasted_iota(jnp.int32, (1, 2 * SPAN), 1) < SPAN
    units = [(h, p) for h in range(PER_STEP) for p in range(CS)]
    lanes = [slice(2 * SPAN * p, 2 * SPAN * (p + 1)) for p in range(CS)]

    def spans_of(kv):
        at = [slice(width * kv + HEAD_DIM * h, width * kv + HEAD_DIM * (h + 1)) for h, _ in units]
        return [
            (kvs[CH_DEV * p][:, a], kvs[CH_DEV * p + 1][:, a]) for (_, p), a in zip(units, at)
        ]

    def both(dot, spans, right):
        return [jnp.where(low, dot(a, r), dot(b, r)) for (a, b), r in zip(spans, right)]

    keys, values = spans_of(0), spans_of(1)
    queries = [qg_ref[h, 0, 0, :, lanes[p]] for h, p in units]
    grads = [qg_ref[h, 0, 1, :, lanes[p]] for h, p in units]
    scores = [s * SCORE_SCALE for s in both(ndot, keys, queries)]
    dprobs = both(ndot, values, grads)
    exponent = [jnp.exp(s - jnp.max(s, axis=0, keepdims=True)) for s in scores]
    probs = [e * (1.0 / jnp.sum(e, axis=0, keepdims=True)) for e in exponent]
    probs_low = [p.astype(jnp.bfloat16) for p in probs]
    outs = [o.astype(jnp.bfloat16) for o in both(tdot, values, probs_low)]
    delta = [
        jnp.sum(g.astype(jnp.float32) * o.astype(jnp.float32), axis=0, keepdims=True)
        for g, o in zip(grads, outs)
    ]
    dscores = [
        (p * (dp - dl) * SCORE_SCALE).astype(jnp.bfloat16)
        for p, dp, dl in zip(probs, dprobs, delta)
    ]
    dqs = [q.astype(jnp.bfloat16) for q in both(tdot, keys, dscores)]
    for i, (h, p) in enumerate(units):
        out_ref[h, 0, :, lanes[p]] = outs[i]
        out_ref[h, 1, :, lanes[p]] = dqs[i]


def attend(place, neighbours, weights, qg):
    steps = HEADS // CS // PER_STEP
    d_steps = steps // 2
    block = (PER_STEP,) + qg.shape[2:]

    def pair_of(i, place):
        return (i + d_steps * place[0]) & (steps - 1)

    def came_at(i, place):
        pair = pair_of(i, place)
        return (pair & (d_steps - 1), jnp.abs(pair // d_steps - place[3] // 2), 0, 0, 0)

    w_block = weights[0].shape[:3] + (PER_STEP * HEAD_DIM,)
    first = pl.BlockSpec(w_block, lambda i, place: (0, 0, 0, jnp.minimum(i, d_steps - 1)))
    last = pl.BlockSpec(w_block, lambda i, place: (0, 0, 0, jnp.maximum(i - d_steps, 0)))
    head_block = pl.BlockSpec(block, lambda i, place: (pair_of(i, place), 0, 0, 0))
    return pl.pallas_call(
        attend_kernel,
        grid_spec=pltpu.PrefetchScalarGridSpec(
            num_scalar_prefetch=1,
            grid=(steps,),
            in_specs=[
                pl.BlockSpec(a.shape, lambda i, place: (0, 0, 0)) for a in neighbours
            ]
            + [first, first, last, last]
            + [pl.BlockSpec(block[:1] + (1,) + block[1:], came_at)],
            out_specs=head_block,
            scratch_shapes=[
                pltpu.VMEM((CS * CH_DEV, NBR * NT, E), jnp.bfloat16),
                pltpu.VMEM((E, 2 * PER_STEP * HEAD_DIM), jnp.bfloat16),
            ],
        ),
        out_shape=jax.ShapeDtypeStruct((CHIPS,) + block[1:], jnp.bfloat16),
        compiler_params=pltpu.CompilerParams(vmem_limit_bytes=40 * 1024 * 1024),
        name="attend",
    )(place, *neighbours, *weights, qg)


def small(queries, cache, cache_scale, w_kv, nbr_shard, nbr_row, grad_out):
    dp_count = lax.axis_size("dp")
    mp_count = lax.axis_size("mp")
    my_dp = lax.axis_index("dp")
    my_mp = lax.axis_index("mp")
    my_c, my_x, my_z = my_mp & 1, (my_mp >> 1) & 1, my_mp >> 2
    place = jnp.stack([my_dp, my_c, my_x, my_z]).astype(jnp.int32)
    slice_len = cache.shape[1]

    def swap(a, bits):
        return lax.ppermute(a, "mp", [(m, m ^ bits) for m in ALL])

    def swap_dp(a):
        return lax.ppermute(a, "dp", [(0, 1), (1, 0)])

    def over_half(a):
        halves = [list(range(HALF)), list(range(HALF, 2 * HALF))]
        return lax.all_to_all(
            a, "mp", split_axis=0, concat_axis=0, tiled=True, axis_index_groups=halves
        )

    turned = [w_kv] + [
        lax.ppermute(w_kv, "mp", [(m, (m + XS * CS * r) % len(ALL)) for m in ALL])
        for r in range(1, ZS)
    ]
    scaled = (cache.astype(jnp.float32) * cache_scale[..., None]).astype(jnp.bfloat16)
    shard_blk, row_blk, slot_blk = requests(nbr_shard, nbr_row, dp_count, mp_count)
    holders = jnp.stack([my_mp, my_mp ^ HALF]).astype(jnp.int32)
    select = jnp.logical_and(
        shard_blk[:, None, None, :] == holders[None, :, None, None],
        slot_blk[:, None, None, :] == jnp.arange(MOST, dtype=jnp.int32)[None, None, :, None],
    )
    wanted = jnp.sum(jnp.where(select, row_blk[:, None, None, :], 0), axis=3)
    wanted = lax.dynamic_slice_in_dim(wanted, my_mp & HALF, HALF, 0)
    near_rows = pick_rows(wanted[:, 0].reshape(-1), scaled)
    scaled, turned, near_rows = lax.optimization_barrier((scaled, turned, near_rows))
    far = swap(scaled, HALF)

    mine, sends = by_parity(my_c.reshape(1).astype(jnp.int32), jnp.concatenate(turned))
    came = swap(sends, 1)
    line_w = jnp.where(
        my_c == 0,
        jnp.concatenate([mine, came], axis=1),
        jnp.concatenate([came, mine], axis=1),
    ).reshape(ZS, 2, CS * w_kv.shape[1], -1)
    x_w, y_w = swap(line_w, CS), swap_dp(line_w)


    shards = lax.dynamic_index_in_dim(shard_blk, my_mp, 0, keepdims=False)
    slots = lax.dynamic_index_in_dim(slot_blk, my_mp, 0, keepdims=False)
    row = jnp.roll(((shards & (HALF - 1)) * MOST + slots).reshape(dp_count, -1), my_dp, 0)
    is_far = jnp.roll(((shards ^ my_mp) & HALF).reshape(dp_count, -1), my_dp, 0)
    row = row.reshape(-1).astype(jnp.int32)
    is_far = is_far.reshape(-1).astype(jnp.int32)

    def spread(rows):
        return over_half(rows.reshape((HALF, MOST) + rows.shape[1:])).reshape(rows.shape)

    near_pieces = spread(near_rows)

    my_half = my_mp // HALF
    chips = CHIPS // 2
    qg = jnp.stack([queries, grad_out]).reshape(2, HEAD_DIM, CHIPS, -1).transpose(2, 0, 1, 3)
    qg = qg.reshape((2, chips) + qg.shape[1:])
    qg_stay = lax.dynamic_index_in_dim(qg, my_half, 0, keepdims=False)
    qg_go = lax.dynamic_index_in_dim(qg, 1 - my_half, 0, keepdims=False)

    far, near_pieces, x_w, y_w, qg_go, row, is_far = lax.optimization_barrier(
        (far, near_pieces, x_w, y_w, qg_go, row, is_far)
    )
    xy_w = swap_dp(x_w)
    far_pieces = spread(pick_rows(wanted[:, 1].reshape(-1), far))
    qg_came = swap(qg_go, HALF)

    far_pieces, qg_came, xy_w = lax.optimization_barrier((far_pieces, qg_came, xy_w))
    chip_lines = [
        [HALF * half + CS * chip + core for chip in range(chips)]
        for half in range(2)
        for core in range(CS)
    ]
    qg = lax.all_to_all(
        jnp.stack([qg_stay, qg_came], axis=1),
        "mp",
        split_axis=0,
        concat_axis=0,
        tiled=True,
        axis_index_groups=chip_lines,
    )
    chip_groups = [[CS * chip + core for chip in range(CHIPS)] for core in range(CS)]

    own, give = choose(
        is_far,
        row,
        near_pieces,
        far_pieces,
    )
    got = swap_dp(give)
    span_shape = (CH_DEV, NBR * slice_len, E)
    own, got = own.reshape(span_shape), got.reshape(span_shape)
    neighbours = (own, got, swap(own, 1), swap(got, 1))

    result = attend(place, neighbours, (line_w, x_w, y_w, xy_w), qg)
    back = lax.all_to_all(
        result, "mp", split_axis=0, concat_axis=0, tiled=True, axis_index_groups=chip_groups
    )
    back = back.transpose(1, 2, 0, 3).reshape((2,) + queries.shape)
    return back[0], back[1]


def general(queries, cache, cache_scale, w_kv, nbr_shard, nbr_row, grad_out):
    dp_count = lax.axis_size("dp")
    mp_count = lax.axis_size("mp")
    my_mp = lax.axis_index("mp")
    slice_len = cache.shape[1]
    most_slots = 2 * ((dp_count * CH_DEV * NBR + mp_count - 1) // mp_count)
    local_query = lax.all_to_all(queries, "mp", split_axis=1, concat_axis=0, tiled=True)
    shard_blk, row_blk, slot_blk = requests(nbr_shard, nbr_row, dp_count, mp_count)
    to_me = shard_blk == my_mp
    slot_ids = jnp.arange(most_slots, dtype=jnp.int32)
    select = jnp.logical_and(to_me[:, None, :], slot_blk[:, None, :] == slot_ids[None, :, None])
    wanted = jnp.sum(jnp.where(select, row_blk[:, None, :], 0), axis=2)
    sending = (cache[wanted].astype(jnp.float32) * cache_scale[wanted][..., None]).astype(
        jnp.bfloat16
    )
    arrived = lax.all_to_all(sending, "mp", split_axis=0, concat_axis=0, tiled=True)
    flat_pieces = arrived.reshape(mp_count * most_slots, slice_len, E)
    own_shards = lax.dynamic_index_in_dim(shard_blk, my_mp, 0, keepdims=False)
    own_slots = lax.dynamic_index_in_dim(slot_blk, my_mp, 0, keepdims=False)
    pieces = jnp.take(flat_pieces, own_shards * most_slots + own_slots, axis=0)
    pieces = pieces.reshape(dp_count, CH_DEV * NBR, slice_len, E)
    gathered = lax.all_to_all(pieces, "dp", split_axis=0, concat_axis=2, tiled=True)
    neighbours = gathered.reshape(CH_DEV, NBR * NT, E)
    gathered_weights = lax.all_gather(w_kv, ("dp", "mp"), axis=0, tiled=False)
    all_weights = (
        gathered_weights.reshape((dp_count, mp_count) + w_kv.shape)
        .transpose(2, 1, 3, 0, 4)
        .reshape(2, E, HEADS * HEAD_DIM)
    )
    key_value = jnp.einsum(
        "cte,ken->kctn", neighbours, all_weights, preferred_element_type=jnp.float32
    ).astype(jnp.bfloat16)
    key_rows = key_value[0].reshape(CH_DEV, NBR * NT, HEADS, HEAD_DIM)
    values = key_value[1].reshape(CH_DEV, NBR * NT, HEADS, HEAD_DIM)
    query_c = local_query.reshape(HEADS, HEAD_DIM, CH_DEV, SPAN)
    affinity_logits = (
        jnp.einsum("hdcq,ckhd->chqk", query_c, key_rows, preferred_element_type=jnp.float32)
        * SCORE_SCALE
    )
    row_max = jnp.max(affinity_logits, axis=3, keepdims=True)
    exponent = jnp.exp(affinity_logits - row_max)
    attn_probs = exponent / jnp.sum(exponent, axis=3, keepdims=True)
    probs_low = attn_probs.astype(jnp.bfloat16)
    output_c = jnp.einsum(
        "chqk,ckhd->hdcq", probs_low, values, preferred_element_type=jnp.float32
    ).astype(jnp.bfloat16)
    output_rows = output_c.reshape(HEADS * HEAD_DIM, CH_DEV * SPAN)
    output_back = lax.all_to_all(output_rows, "mp", split_axis=0, concat_axis=1, tiled=True)
    local_grad = lax.all_to_all(grad_out, "mp", split_axis=1, concat_axis=0, tiled=True)
    grad_c = local_grad.reshape(HEADS, HEAD_DIM, CH_DEV, SPAN)
    dprobs = jnp.einsum("hdcq,ckhd->chqk", grad_c, values, preferred_element_type=jnp.float32)
    row_delta = jnp.einsum("hdcq,hdcq->chq", grad_c, output_c, preferred_element_type=jnp.float32)
    dscores = (attn_probs * (dprobs - row_delta[..., None]) * SCORE_SCALE).astype(jnp.bfloat16)
    grad_query = jnp.einsum(
        "chqk,ckhd->hdcq", dscores, key_rows, preferred_element_type=jnp.float32
    ).astype(jnp.bfloat16)
    grad_rows = grad_query.reshape(HEADS * HEAD_DIM, CH_DEV * SPAN)
    grad_back = lax.all_to_all(grad_rows, "mp", split_axis=0, concat_axis=1, tiled=True)
    return (output_back, grad_back)


def solution(mesh):
    fits = mesh.shape["dp"] == 2 and mesh.shape["mp"] == len(ALL)
    return jax.shard_map(
        small if fits else general,
        mesh=mesh,
        in_specs=(
            P("mp", "dp"),
            P("mp", "dp", None),
            P("mp", "dp"),
            P(None, "mp", "dp"),
            P(),
            P(),
            P("mp", "dp"),
        ),
        out_specs=(P("mp", "dp"), P("mp", "dp")),
        check_vma=False,
    )
```

```python
import jax
import jax.numpy as jnp
from jax import lax
from jax.experimental import pallas as pl
from jax.experimental.pallas import tpu as pltpu
from jax.sharding import PartitionSpec as P

HEADS = 16
HEAD_DIM = 128
E = 896
NT = 128
SPAN = 64
NBR = 2
CH_DEV = 2
MOST = 2

SCORE_SCALE = HEAD_DIM ** (-0.5)


def requests(nbr_shard, nbr_row, dp_count, mp_count):
    block_size = dp_count * CH_DEV * NBR
    shard_blk = (
        nbr_shard.reshape(dp_count, mp_count, CH_DEV * NBR)
        .transpose(1, 0, 2)
        .reshape(mp_count, block_size)
    )
    row_blk = (
        nbr_row.reshape(dp_count, mp_count, CH_DEV * NBR)
        .transpose(1, 0, 2)
        .reshape(mp_count, block_size)
    )
    positions = jnp.arange(block_size, dtype=jnp.int32)
    earlier = positions[None, :] < positions[:, None]
    same_shard = shard_blk[:, :, None] == shard_blk[:, None, :]
    slot_blk = jnp.sum(jnp.logical_and(same_shard, earlier[None]), axis=2)
    return shard_blk, row_blk, slot_blk


ZS, XS, CS = 4, 2, 2
CHIPS = ZS * XS
HALF = 8
PER_STEP = 4
ALL = range(ZS * XS * CS)


def parity_kernel(core_ref, w_ref, mine_ref, sends_ref):
    for core in range(CS):

        @pl.when(core_ref[0] == core)
        def _():
            for j in range(HEADS // CS // 2):
                at = slice(j * HEAD_DIM, (j + 1) * HEAD_DIM)
                for ref, parity in ((mine_ref, core), (sends_ref, 1 - core)):
                    head = CS * j + parity
                    ref[:, :, at] = w_ref[:, :, head * HEAD_DIM : (head + 1) * HEAD_DIM]


def by_parity(core, w_kv):
    half = jax.ShapeDtypeStruct(w_kv.shape[:2] + (w_kv.shape[2] // CS,), w_kv.dtype)
    return pl.pallas_call(
        parity_kernel,
        in_specs=[
            pl.BlockSpec(memory_space=pltpu.SMEM),
            pl.BlockSpec(memory_space=pltpu.VMEM),
        ],
        out_specs=[pl.BlockSpec(memory_space=pltpu.VMEM)] * 2,
        out_shape=[half] * 2,
        name="by_parity",
    )(core, w_kv)


def rows_kernel(rows_ref, src_ref, out_ref):
    for k in range(out_ref.shape[0]):
        out_ref[k] = src_ref[rows_ref[k]]


def pick_rows(rows, source):
    return pl.pallas_call(
        rows_kernel,
        in_specs=[
            pl.BlockSpec(memory_space=pltpu.SMEM),
            pl.BlockSpec(memory_space=pltpu.VMEM),
        ],
        out_specs=pl.BlockSpec(memory_space=pltpu.VMEM),
        out_shape=jax.ShapeDtypeStruct(rows.shape + source.shape[1:], source.dtype),
        compiler_params=pltpu.CompilerParams(vmem_limit_bytes=32 * 1024 * 1024),
        name="pick_rows",
    )(rows, source)


def choose_kernel(far_ref, row_ref, near, far, own, give, sem):
    each = CH_DEV * NBR
    outs = [(own if r < each else give).at[r % each] for r in range(2 * each)]
    for r, out in enumerate(outs):

        @pl.when(far_ref[r] == 0)
        def _():
            pltpu.make_async_copy(near.at[row_ref[r]], out, sem.at[r]).start()

        @pl.when(far_ref[r] != 0)
        def _():
            pltpu.make_async_copy(far.at[row_ref[r]], out, sem.at[r]).start()

    for r, out in enumerate(outs):
        pltpu.make_async_copy(near.at[0], out, sem.at[r]).wait()


def choose(is_far, row, near, far):
    half = jax.ShapeDtypeStruct((CH_DEV * NBR,) + near.shape[1:], near.dtype)
    return pl.pallas_call(
        choose_kernel,
        in_specs=[pl.BlockSpec(memory_space=pltpu.SMEM)] * 2
        + [pl.BlockSpec(memory_space=pl.ANY)] * 2,
        out_specs=[pl.BlockSpec(memory_space=pltpu.VMEM)] * 2,
        out_shape=[half] * 2,
        scratch_shapes=[pltpu.SemaphoreType.DMA((2 * CH_DEV * NBR,))],
        name="choose",
    )(is_far, row, near, far)


def tdot(a, b):
    return lax.dot_general(a, b, (((0,), (0,)), ((), ())), preferred_element_type=jnp.float32)


def ndot(a, b):
    return jnp.dot(a, b, preferred_element_type=jnp.float32)


def attend_kernel(
    place_ref, na, nb, sa, sb, w_own, w_x, w_y, w_xy, qg_ref, out_ref, n_scr, w_scr
):
    my_c, my_x, my_z = place_ref[1], place_ref[2], place_ref[3]
    rows, width = w_scr.shape[0] // CHIPS, w_scr.shape[1] // 2

    @pl.when(pl.program_id(0) == 0)
    def _():
        for s in range(CH_DEV):
            for core, first, second in ((my_c, na, nb), (1 - my_c, sa, sb)):
                n_scr[CH_DEV * core + s, 0:NT, :] = first[s]
                n_scr[CH_DEV * core + s, NT : 2 * NT, :] = second[s]

    def put(*sources):
        for r in range(ZS):
            src_z = lax.rem(my_z - r + ZS, ZS)
            for other, ref in enumerate(sources):
                at = pl.multiple_of((src_z * XS + (my_x ^ other)) * rows, 16)
                for kv in range(2):
                    lanes = slice(width * kv, width * (kv + 1))
                    w_scr[pl.ds(at, rows), lanes] = ref[r, kv]

    own_dp = pl.program_id(0) < pl.num_programs(0) // 2

    @pl.when(own_dp)
    def _():
        put(w_own, w_x)

    @pl.when(jnp.logical_not(own_dp))
    def _():
        put(w_y, w_xy)

    weights = w_scr[...]
    kvs = [ndot(n_scr[s], weights).astype(jnp.bfloat16) for s in range(CS * CH_DEV)]
    low = lax.broadcasted_iota(jnp.int32, (1, 2 * SPAN), 1) < SPAN
    units = [(h, p) for h in range(PER_STEP) for p in range(CS)]
    lanes = [slice(2 * SPAN * p, 2 * SPAN * (p + 1)) for p in range(CS)]

    def spans_of(kv):
        at = [slice(width * kv + HEAD_DIM * h, width * kv + HEAD_DIM * (h + 1)) for h, _ in units]
        return [
            (kvs[CH_DEV * p][:, a], kvs[CH_DEV * p + 1][:, a]) for (_, p), a in zip(units, at)
        ]

    def both(dot, spans, right):
        return [jnp.where(low, dot(a, r), dot(b, r)) for (a, b), r in zip(spans, right)]

    keys, values = spans_of(0), spans_of(1)
    queries = [qg_ref[h, 0, 0, :, lanes[p]] for h, p in units]
    grads = [qg_ref[h, 0, 1, :, lanes[p]] for h, p in units]
    scores = [s * SCORE_SCALE for s in both(ndot, keys, queries)]
    dprobs = both(ndot, values, grads)
    exponent = [jnp.exp(s - jnp.max(s, axis=0, keepdims=True)) for s in scores]
    probs = [e * (1.0 / jnp.sum(e, axis=0, keepdims=True)) for e in exponent]
    probs_low = [p.astype(jnp.bfloat16) for p in probs]
    outs = [o.astype(jnp.bfloat16) for o in both(tdot, values, probs_low)]
    delta = [
        jnp.sum(g.astype(jnp.float32) * o.astype(jnp.float32), axis=0, keepdims=True)
        for g, o in zip(grads, outs)
    ]
    dscores = [
        (p * (dp - dl) * SCORE_SCALE).astype(jnp.bfloat16)
        for p, dp, dl in zip(probs, dprobs, delta)
    ]
    dqs = [q.astype(jnp.bfloat16) for q in both(tdot, keys, dscores)]
    for i, (h, p) in enumerate(units):
        out_ref[h, 0, :, lanes[p]] = outs[i]
        out_ref[h, 1, :, lanes[p]] = dqs[i]


def attend(place, neighbours, weights, qg):
    steps = HEADS // CS // PER_STEP
    d_steps = steps // 2
    block = (PER_STEP,) + qg.shape[2:]

    def pair_of(i, place):
        return (i + d_steps * place[0]) & (steps - 1)

    def came_at(i, place):
        pair = pair_of(i, place)
        return (pair & (d_steps - 1), jnp.abs(pair // d_steps - place[3] // 2), 0, 0, 0)

    w_block = weights[0].shape[:3] + (PER_STEP * HEAD_DIM,)
    first = pl.BlockSpec(w_block, lambda i, place: (0, 0, 0, jnp.minimum(i, d_steps - 1)))
    last = pl.BlockSpec(w_block, lambda i, place: (0, 0, 0, jnp.maximum(i - d_steps, 0)))
    head_block = pl.BlockSpec(block, lambda i, place: (pair_of(i, place), 0, 0, 0))
    return pl.pallas_call(
        attend_kernel,
        grid_spec=pltpu.PrefetchScalarGridSpec(
            num_scalar_prefetch=1,
            grid=(steps,),
            in_specs=[
                pl.BlockSpec(a.shape, lambda i, place: (0, 0, 0)) for a in neighbours
            ]
            + [first, first, last, last]
            + [pl.BlockSpec(block[:1] + (1,) + block[1:], came_at)],
            out_specs=head_block,
            scratch_shapes=[
                pltpu.VMEM((CS * CH_DEV, NBR * NT, E), jnp.bfloat16),
                pltpu.VMEM((E, 2 * PER_STEP * HEAD_DIM), jnp.bfloat16),
            ],
        ),
        out_shape=jax.ShapeDtypeStruct((CHIPS,) + block[1:], jnp.bfloat16),
        compiler_params=pltpu.CompilerParams(vmem_limit_bytes=40 * 1024 * 1024),
        name="attend",
    )(place, *neighbours, *weights, qg)


def small(queries, cache, cache_scale, w_kv, nbr_shard, nbr_row, grad_out):
    dp_count = lax.axis_size("dp")
    mp_count = lax.axis_size("mp")
    my_dp = lax.axis_index("dp")
    my_mp = lax.axis_index("mp")
    my_c, my_x, my_z = my_mp & 1, (my_mp >> 1) & 1, my_mp >> 2
    place = jnp.stack([my_dp, my_c, my_x, my_z]).astype(jnp.int32)
    slice_len = cache.shape[1]

    def swap(a, bits):
        return lax.ppermute(a, "mp", [(m, m ^ bits) for m in ALL])

    def swap_dp(a):
        return lax.ppermute(a, "dp", [(0, 1), (1, 0)])

    def over_half(a):
        halves = [list(range(HALF)), list(range(HALF, 2 * HALF))]
        return lax.all_to_all(
            a, "mp", split_axis=0, concat_axis=0, tiled=True, axis_index_groups=halves
        )

    turned = [w_kv] + [
        lax.ppermute(w_kv, "mp", [(m, (m + XS * CS * r) % len(ALL)) for m in ALL])
        for r in range(1, ZS)
    ]
    scaled = (cache.astype(jnp.float32) * cache_scale[..., None]).astype(jnp.bfloat16)
    shard_blk, row_blk, slot_blk = requests(nbr_shard, nbr_row, dp_count, mp_count)
    holders = jnp.stack([my_mp, my_mp ^ HALF]).astype(jnp.int32)
    select = jnp.logical_and(
        shard_blk[:, None, None, :] == holders[None, :, None, None],
        slot_blk[:, None, None, :] == jnp.arange(MOST, dtype=jnp.int32)[None, None, :, None],
    )
    wanted = jnp.sum(jnp.where(select, row_blk[:, None, None, :], 0), axis=3)
    wanted = lax.dynamic_slice_in_dim(wanted, my_mp & HALF, HALF, 0)
    my_half = my_mp // HALF
    chips = CHIPS // 2
    qg = jnp.stack([queries, grad_out]).reshape(2, HEAD_DIM, CHIPS, -1).transpose(2, 0, 1, 3)
    qg = qg.reshape((2, chips) + qg.shape[1:])
    qg_stay = lax.dynamic_index_in_dim(qg, my_half, 0, keepdims=False)
    qg_go = lax.dynamic_index_in_dim(qg, 1 - my_half, 0, keepdims=False)
    near_rows = pick_rows(wanted[:, 0].reshape(-1), scaled)
    scaled, turned, near_rows, qg_go, qg_stay = lax.optimization_barrier(
        (scaled, turned, near_rows, qg_go, qg_stay)
    )
    far = swap(scaled, HALF)

    core = my_c.reshape(1).astype(jnp.int32)

    def parity_rows(line):
        mine, sends = by_parity(core, line)
        came = swap(sends, 1)
        return jnp.where(
            my_c == 0,
            jnp.concatenate([mine, came], axis=1),
            jnp.concatenate([came, mine], axis=1),
        ).reshape(ZS, 2, CS * w_kv.shape[1], -1)

    line = jnp.concatenate(turned)
    x_line, y_line = swap(line, CS), swap_dp(line)

    shards = lax.dynamic_index_in_dim(shard_blk, my_mp, 0, keepdims=False)
    slots = lax.dynamic_index_in_dim(slot_blk, my_mp, 0, keepdims=False)
    row = jnp.roll(((shards & (HALF - 1)) * MOST + slots).reshape(dp_count, -1), my_dp, 0)
    is_far = jnp.roll(((shards ^ my_mp) & HALF).reshape(dp_count, -1), my_dp, 0)
    row = row.reshape(-1).astype(jnp.int32)
    is_far = is_far.reshape(-1).astype(jnp.int32)

    def spread(rows):
        return over_half(rows.reshape((HALF, MOST) + rows.shape[1:])).reshape(rows.shape)

    near_pieces = spread(near_rows)

    line_w = parity_rows(line)
    far, near_pieces, x_line, y_line, line_w, row, is_far = lax.optimization_barrier(
        (far, near_pieces, x_line, y_line, line_w, row, is_far)
    )
    xy_line = swap_dp(x_line)
    x_w, y_w = parity_rows(x_line), parity_rows(y_line)
    far_pieces = spread(pick_rows(wanted[:, 1].reshape(-1), far))
    qg_came = swap(qg_go, HALF)

    far_pieces, qg_came, xy_line, x_w, y_w = lax.optimization_barrier(
        (far_pieces, qg_came, xy_line, x_w, y_w)
    )
    xy_w = parity_rows(xy_line)
    chip_lines = [
        [HALF * half + CS * chip + core for chip in range(chips)]
        for half in range(2)
        for core in range(CS)
    ]
    chip_groups = [[CS * chip + core for chip in range(CHIPS)] for core in range(CS)]

    own, give = choose(
        is_far,
        row,
        near_pieces,
        far_pieces,
    )
    give, qg_came = lax.optimization_barrier((give, qg_came))
    got = swap_dp(give)
    qg = lax.all_to_all(
        jnp.stack([qg_stay, qg_came], axis=1),
        "mp",
        split_axis=0,
        concat_axis=0,
        tiled=True,
        axis_index_groups=chip_lines,
    )
    span_shape = (CH_DEV, NBR * slice_len, E)
    own, got = own.reshape(span_shape), got.reshape(span_shape)
    neighbours = (own, got, swap(own, 1), swap(got, 1))

    result = attend(place, neighbours, (line_w, x_w, y_w, xy_w), qg)
    back = lax.all_to_all(
        result, "mp", split_axis=0, concat_axis=0, tiled=True, axis_index_groups=chip_groups
    )
    back = back.transpose(1, 2, 0, 3).reshape((2,) + queries.shape)
    return back[0], back[1]


def general(queries, cache, cache_scale, w_kv, nbr_shard, nbr_row, grad_out):
    dp_count = lax.axis_size("dp")
    mp_count = lax.axis_size("mp")
    my_mp = lax.axis_index("mp")
    slice_len = cache.shape[1]
    most_slots = 2 * ((dp_count * CH_DEV * NBR + mp_count - 1) // mp_count)
    local_query = lax.all_to_all(queries, "mp", split_axis=1, concat_axis=0, tiled=True)
    shard_blk, row_blk, slot_blk = requests(nbr_shard, nbr_row, dp_count, mp_count)
    to_me = shard_blk == my_mp
    slot_ids = jnp.arange(most_slots, dtype=jnp.int32)
    select = jnp.logical_and(to_me[:, None, :], slot_blk[:, None, :] == slot_ids[None, :, None])
    wanted = jnp.sum(jnp.where(select, row_blk[:, None, :], 0), axis=2)
    sending = (cache[wanted].astype(jnp.float32) * cache_scale[wanted][..., None]).astype(
        jnp.bfloat16
    )
    arrived = lax.all_to_all(sending, "mp", split_axis=0, concat_axis=0, tiled=True)
    flat_pieces = arrived.reshape(mp_count * most_slots, slice_len, E)
    own_shards = lax.dynamic_index_in_dim(shard_blk, my_mp, 0, keepdims=False)
    own_slots = lax.dynamic_index_in_dim(slot_blk, my_mp, 0, keepdims=False)
    pieces = jnp.take(flat_pieces, own_shards * most_slots + own_slots, axis=0)
    pieces = pieces.reshape(dp_count, CH_DEV * NBR, slice_len, E)
    gathered = lax.all_to_all(pieces, "dp", split_axis=0, concat_axis=2, tiled=True)
    neighbours = gathered.reshape(CH_DEV, NBR * NT, E)
    gathered_weights = lax.all_gather(w_kv, ("dp", "mp"), axis=0, tiled=False)
    all_weights = (
        gathered_weights.reshape((dp_count, mp_count) + w_kv.shape)
        .transpose(2, 1, 3, 0, 4)
        .reshape(2, E, HEADS * HEAD_DIM)
    )
    key_value = jnp.einsum(
        "cte,ken->kctn", neighbours, all_weights, preferred_element_type=jnp.float32
    ).astype(jnp.bfloat16)
    key_rows = key_value[0].reshape(CH_DEV, NBR * NT, HEADS, HEAD_DIM)
    values = key_value[1].reshape(CH_DEV, NBR * NT, HEADS, HEAD_DIM)
    query_c = local_query.reshape(HEADS, HEAD_DIM, CH_DEV, SPAN)
    affinity_logits = (
        jnp.einsum("hdcq,ckhd->chqk", query_c, key_rows, preferred_element_type=jnp.float32)
        * SCORE_SCALE
    )
    row_max = jnp.max(affinity_logits, axis=3, keepdims=True)
    exponent = jnp.exp(affinity_logits - row_max)
    attn_probs = exponent / jnp.sum(exponent, axis=3, keepdims=True)
    probs_low = attn_probs.astype(jnp.bfloat16)
    output_c = jnp.einsum(
        "chqk,ckhd->hdcq", probs_low, values, preferred_element_type=jnp.float32
    ).astype(jnp.bfloat16)
    output_rows = output_c.reshape(HEADS * HEAD_DIM, CH_DEV * SPAN)
    output_back = lax.all_to_all(output_rows, "mp", split_axis=0, concat_axis=1, tiled=True)
    local_grad = lax.all_to_all(grad_out, "mp", split_axis=1, concat_axis=0, tiled=True)
    grad_c = local_grad.reshape(HEADS, HEAD_DIM, CH_DEV, SPAN)
    dprobs = jnp.einsum("hdcq,ckhd->chqk", grad_c, values, preferred_element_type=jnp.float32)
    row_delta = jnp.einsum("hdcq,hdcq->chq", grad_c, output_c, preferred_element_type=jnp.float32)
    dscores = (attn_probs * (dprobs - row_delta[..., None]) * SCORE_SCALE).astype(jnp.bfloat16)
    grad_query = jnp.einsum(
        "chqk,ckhd->hdcq", dscores, key_rows, preferred_element_type=jnp.float32
    ).astype(jnp.bfloat16)
    grad_rows = grad_query.reshape(HEADS * HEAD_DIM, CH_DEV * SPAN)
    grad_back = lax.all_to_all(grad_rows, "mp", split_axis=0, concat_axis=1, tiled=True)
    return (output_back, grad_back)


def solution(mesh):
    fits = mesh.shape["dp"] == 2 and mesh.shape["mp"] == len(ALL)
    return jax.shard_map(
        small if fits else general,
        mesh=mesh,
        in_specs=(
            P("mp", "dp"),
            P("mp", "dp", None),
            P("mp", "dp"),
            P(None, "mp", "dp"),
            P(),
            P(),
            P("mp", "dp"),
        ),
        out_specs=(P("mp", "dp"), P("mp", "dp")),
        check_vma=False,
    )
```

```python
import jax
import jax.numpy as jnp
from jax import lax
from jax.experimental import pallas as pl
from jax.experimental.pallas import tpu as pltpu
from jax.sharding import PartitionSpec as P

HEADS = 16
HEAD_DIM = 128
E = 896
NT = 128
SPAN = 64
NBR = 2
CH_DEV = 2
MOST = 2

SCORE_SCALE = HEAD_DIM ** (-0.5)


def requests(nbr_shard, nbr_row, dp_count, mp_count):
    block_size = dp_count * CH_DEV * NBR
    shard_blk = (
        nbr_shard.reshape(dp_count, mp_count, CH_DEV * NBR)
        .transpose(1, 0, 2)
        .reshape(mp_count, block_size)
    )
    row_blk = (
        nbr_row.reshape(dp_count, mp_count, CH_DEV * NBR)
        .transpose(1, 0, 2)
        .reshape(mp_count, block_size)
    )
    positions = jnp.arange(block_size, dtype=jnp.int32)
    earlier = positions[None, :] < positions[:, None]
    same_shard = shard_blk[:, :, None] == shard_blk[:, None, :]
    slot_blk = jnp.sum(jnp.logical_and(same_shard, earlier[None]), axis=2)
    return shard_blk, row_blk, slot_blk


ZS, XS, CS = 4, 2, 2
CHIPS = ZS * XS
HALF = 8
PER_STEP = 4
ALL = range(ZS * XS * CS)


def parity_kernel(core_ref, w_ref, mine_ref, sends_ref):
    for core in range(CS):

        @pl.when(core_ref[0] == core)
        def _():
            for j in range(HEADS // CS // 2):
                at = slice(j * HEAD_DIM, (j + 1) * HEAD_DIM)
                for ref, parity in ((mine_ref, core), (sends_ref, 1 - core)):
                    head = CS * j + parity
                    ref[:, :, at] = w_ref[:, :, head * HEAD_DIM : (head + 1) * HEAD_DIM]


def by_parity(core, w_kv):
    half = jax.ShapeDtypeStruct(w_kv.shape[:2] + (w_kv.shape[2] // CS,), w_kv.dtype)
    return pl.pallas_call(
        parity_kernel,
        in_specs=[
            pl.BlockSpec(memory_space=pltpu.SMEM),
            pl.BlockSpec(memory_space=pltpu.VMEM),
        ],
        out_specs=[pl.BlockSpec(memory_space=pltpu.VMEM)] * 2,
        out_shape=[half] * 2,
        name="by_parity",
    )(core, w_kv)


def rows_kernel(rows_ref, src_ref, out_ref):
    for k in range(out_ref.shape[0]):
        out_ref[k] = src_ref[rows_ref[k]]


def pick_rows(rows, source):
    return pl.pallas_call(
        rows_kernel,
        in_specs=[
            pl.BlockSpec(memory_space=pltpu.SMEM),
            pl.BlockSpec(memory_space=pltpu.VMEM),
        ],
        out_specs=pl.BlockSpec(memory_space=pltpu.VMEM),
        out_shape=jax.ShapeDtypeStruct(rows.shape + source.shape[1:], source.dtype),
        compiler_params=pltpu.CompilerParams(vmem_limit_bytes=32 * 1024 * 1024),
        name="pick_rows",
    )(rows, source)


def choose_kernel(far_ref, row_ref, near, far, own, give, sem):
    each = CH_DEV * NBR
    outs = [(own if r < each else give).at[r % each] for r in range(2 * each)]
    for r, out in enumerate(outs):

        @pl.when(far_ref[r] == 0)
        def _():
            pltpu.make_async_copy(near.at[row_ref[r]], out, sem.at[r]).start()

        @pl.when(far_ref[r] != 0)
        def _():
            pltpu.make_async_copy(far.at[row_ref[r]], out, sem.at[r]).start()

    for r, out in enumerate(outs):
        pltpu.make_async_copy(near.at[0], out, sem.at[r]).wait()


def choose(is_far, row, near, far):
    half = jax.ShapeDtypeStruct((CH_DEV * NBR,) + near.shape[1:], near.dtype)
    return pl.pallas_call(
        choose_kernel,
        in_specs=[pl.BlockSpec(memory_space=pltpu.SMEM)] * 2
        + [pl.BlockSpec(memory_space=pl.ANY)] * 2,
        out_specs=[pl.BlockSpec(memory_space=pltpu.VMEM)] * 2,
        out_shape=[half] * 2,
        scratch_shapes=[pltpu.SemaphoreType.DMA((2 * CH_DEV * NBR,))],
        name="choose",
    )(is_far, row, near, far)


def tdot(a, b):
    return lax.dot_general(a, b, (((0,), (0,)), ((), ())), preferred_element_type=jnp.float32)


def ndot(a, b):
    return jnp.dot(a, b, preferred_element_type=jnp.float32)


def attend_kernel(
    place_ref, na, nb, sa, sb, w_own, w_x, w_y, mine, came, qg_ref, out_ref, n_scr, w_scr
):
    my_c, my_x, my_z = place_ref[1], place_ref[2], place_ref[3]
    rows, width = w_scr.shape[0] // CHIPS, w_scr.shape[1] // 2

    @pl.when(pl.program_id(0) == 0)
    def _():
        for s in range(CH_DEV):
            for core, first, second in ((my_c, na, nb), (1 - my_c, sa, sb)):
                n_scr[CH_DEV * core + s, 0:NT, :] = first[s]
                n_scr[CH_DEV * core + s, NT : 2 * NT, :] = second[s]

    def spot(r, other):
        src_z = lax.rem(my_z - r + ZS, ZS)
        return pl.ds(pl.multiple_of((src_z * XS + (my_x ^ other)) * rows, 16), rows)

    def put(ref, other):
        for r in range(ZS):
            for kv in range(2):
                w_scr[spot(r, other), width * kv : width * (kv + 1)] = ref[r, kv]

    def put_parts(other):
        for r in range(ZS):
            for kv in range(2):
                m, c = (a[2 * r + kv].astype(jnp.float32) for a in (mine, came))
                both_rows = [jnp.where(my_c == 0, m, c), jnp.where(my_c == 0, c, m)]
                block = jnp.concatenate(both_rows, axis=0).astype(jnp.bfloat16)
                w_scr[spot(r, other), width * kv : width * (kv + 1)] = block

    own_dp = pl.program_id(0) < pl.num_programs(0) // 2

    @pl.when(own_dp)
    def _():
        put(w_own, 0)
        put(w_x, 1)

    @pl.when(jnp.logical_not(own_dp))
    def _():
        put(w_y, 0)
        put_parts(1)

    weights = w_scr[...]
    kvs = [ndot(n_scr[s], weights).astype(jnp.bfloat16) for s in range(CS * CH_DEV)]
    low = lax.broadcasted_iota(jnp.int32, (1, 2 * SPAN), 1) < SPAN
    units = [(h, p) for h in range(PER_STEP) for p in range(CS)]
    lanes = [slice(2 * SPAN * p, 2 * SPAN * (p + 1)) for p in range(CS)]

    def spans_of(kv):
        at = [slice(width * kv + HEAD_DIM * h, width * kv + HEAD_DIM * (h + 1)) for h, _ in units]
        return [
            (kvs[CH_DEV * p][:, a], kvs[CH_DEV * p + 1][:, a]) for (_, p), a in zip(units, at)
        ]

    def both(dot, spans, right):
        return [jnp.where(low, dot(a, r), dot(b, r)) for (a, b), r in zip(spans, right)]

    keys, values = spans_of(0), spans_of(1)
    queries = [qg_ref[h, 0, 0, :, lanes[p]] for h, p in units]
    grads = [qg_ref[h, 0, 1, :, lanes[p]] for h, p in units]
    scores = [s * SCORE_SCALE for s in both(ndot, keys, queries)]
    dprobs = both(ndot, values, grads)
    exponent = [jnp.exp(s - jnp.max(s, axis=0, keepdims=True)) for s in scores]
    probs = [e * (1.0 / jnp.sum(e, axis=0, keepdims=True)) for e in exponent]
    probs_low = [p.astype(jnp.bfloat16) for p in probs]
    outs = [o.astype(jnp.bfloat16) for o in both(tdot, values, probs_low)]
    delta = [
        jnp.sum(g.astype(jnp.float32) * o.astype(jnp.float32), axis=0, keepdims=True)
        for g, o in zip(grads, outs)
    ]
    dscores = [
        (p * (dp - dl) * SCORE_SCALE).astype(jnp.bfloat16)
        for p, dp, dl in zip(probs, dprobs, delta)
    ]
    dqs = [q.astype(jnp.bfloat16) for q in both(tdot, keys, dscores)]
    for i, (h, p) in enumerate(units):
        out_ref[h, 0, :, lanes[p]] = outs[i]
        out_ref[h, 1, :, lanes[p]] = dqs[i]


def attend(place, neighbours, weights, qg):
    steps = HEADS // CS // PER_STEP
    d_steps = steps // 2
    block = (PER_STEP,) + qg.shape[2:]

    def pair_of(i, place):
        return (i + d_steps * place[0]) & (steps - 1)

    def came_at(i, place):
        pair = pair_of(i, place)
        return (pair & (d_steps - 1), jnp.abs(pair // d_steps - place[3] // 2), 0, 0, 0)

    w_block = weights[0].shape[:3] + (PER_STEP * HEAD_DIM,)
    first = pl.BlockSpec(w_block, lambda i, place: (0, 0, 0, jnp.minimum(i, d_steps - 1)))
    last = pl.BlockSpec(w_block, lambda i, place: (0, 0, 0, jnp.maximum(i - d_steps, 0)))
    head_block = pl.BlockSpec(block, lambda i, place: (pair_of(i, place), 0, 0, 0))
    return pl.pallas_call(
        attend_kernel,
        grid_spec=pltpu.PrefetchScalarGridSpec(
            num_scalar_prefetch=1,
            grid=(steps,),
            in_specs=[
                pl.BlockSpec(a.shape, lambda i, place: (0, 0, 0)) for a in neighbours
            ]
            + [first, first, last]
            + [pl.BlockSpec(a.shape, lambda i, place: (0, 0, 0)) for a in weights[3:]]
            + [pl.BlockSpec(block[:1] + (1,) + block[1:], came_at)],
            out_specs=head_block,
            scratch_shapes=[
                pltpu.VMEM((CS * CH_DEV, NBR * NT, E), jnp.bfloat16),
                pltpu.VMEM((E, 2 * PER_STEP * HEAD_DIM), jnp.bfloat16),
            ],
        ),
        out_shape=jax.ShapeDtypeStruct((CHIPS,) + block[1:], jnp.bfloat16),
        compiler_params=pltpu.CompilerParams(vmem_limit_bytes=40 * 1024 * 1024),
        name="attend",
    )(place, *neighbours, *weights, qg)


def small(queries, cache, cache_scale, w_kv, nbr_shard, nbr_row, grad_out):
    dp_count = lax.axis_size("dp")
    mp_count = lax.axis_size("mp")
    my_dp = lax.axis_index("dp")
    my_mp = lax.axis_index("mp")
    my_c, my_x, my_z = my_mp & 1, (my_mp >> 1) & 1, my_mp >> 2
    place = jnp.stack([my_dp, my_c, my_x, my_z]).astype(jnp.int32)
    slice_len = cache.shape[1]

    def swap(a, bits):
        return lax.ppermute(a, "mp", [(m, m ^ bits) for m in ALL])

    def swap_dp(a):
        return lax.ppermute(a, "dp", [(0, 1), (1, 0)])

    def over_half(a):
        halves = [list(range(HALF)), list(range(HALF, 2 * HALF))]
        return lax.all_to_all(
            a, "mp", split_axis=0, concat_axis=0, tiled=True, axis_index_groups=halves
        )

    turned = [w_kv] + [
        lax.ppermute(w_kv, "mp", [(m, (m + XS * CS * r) % len(ALL)) for m in ALL])
        for r in range(1, ZS)
    ]
    scaled = (cache.astype(jnp.float32) * cache_scale[..., None]).astype(jnp.bfloat16)
    shard_blk, row_blk, slot_blk = requests(nbr_shard, nbr_row, dp_count, mp_count)
    holders = jnp.stack([my_mp, my_mp ^ HALF]).astype(jnp.int32)
    select = jnp.logical_and(
        shard_blk[:, None, None, :] == holders[None, :, None, None],
        slot_blk[:, None, None, :] == jnp.arange(MOST, dtype=jnp.int32)[None, None, :, None],
    )
    wanted = jnp.sum(jnp.where(select, row_blk[:, None, None, :], 0), axis=3)
    wanted = lax.dynamic_slice_in_dim(wanted, my_mp & HALF, HALF, 0)
    my_half = my_mp // HALF
    chips = CHIPS // 2
    qg = jnp.stack([queries, grad_out]).reshape(2, HEAD_DIM, CHIPS, -1).transpose(2, 0, 1, 3)
    qg = qg.reshape((2, chips) + qg.shape[1:])
    qg_stay = lax.dynamic_index_in_dim(qg, my_half, 0, keepdims=False)
    qg_go = lax.dynamic_index_in_dim(qg, 1 - my_half, 0, keepdims=False)
    near_rows = pick_rows(wanted[:, 0].reshape(-1), scaled)
    scaled, turned, near_rows, qg_go, qg_stay = lax.optimization_barrier(
        (scaled, turned, near_rows, qg_go, qg_stay)
    )
    far = swap(scaled, HALF)

    core = my_c.reshape(1).astype(jnp.int32)

    def parity_rows(line):
        mine, sends = by_parity(core, line)
        came = swap(sends, 1)
        return jnp.where(
            my_c == 0,
            jnp.concatenate([mine, came], axis=1),
            jnp.concatenate([came, mine], axis=1),
        ).reshape(ZS, 2, CS * w_kv.shape[1], -1)

    line = jnp.concatenate(turned)
    x_line, y_line = swap(line, CS), swap_dp(line)

    shards = lax.dynamic_index_in_dim(shard_blk, my_mp, 0, keepdims=False)
    slots = lax.dynamic_index_in_dim(slot_blk, my_mp, 0, keepdims=False)
    row = jnp.roll(((shards & (HALF - 1)) * MOST + slots).reshape(dp_count, -1), my_dp, 0)
    is_far = jnp.roll(((shards ^ my_mp) & HALF).reshape(dp_count, -1), my_dp, 0)
    row = row.reshape(-1).astype(jnp.int32)
    is_far = is_far.reshape(-1).astype(jnp.int32)

    def spread(rows):
        return over_half(rows.reshape((HALF, MOST) + rows.shape[1:])).reshape(rows.shape)

    near_pieces = spread(near_rows)

    line_w = parity_rows(line)
    far, near_pieces, x_line, y_line, line_w, row, is_far = lax.optimization_barrier(
        (far, near_pieces, x_line, y_line, line_w, row, is_far)
    )
    xy_line = swap_dp(x_line)
    x_w, y_w = parity_rows(x_line), parity_rows(y_line)
    far_pieces = spread(pick_rows(wanted[:, 1].reshape(-1), far))
    qg_came = swap(qg_go, HALF)

    far_pieces, qg_came, xy_line, x_w, y_w = lax.optimization_barrier(
        (far_pieces, qg_came, xy_line, x_w, y_w)
    )
    xy_mine, xy_sends = by_parity(core, xy_line)
    xy_came = swap(xy_sends, 1)
    chip_lines = [
        [HALF * half + CS * chip + core for chip in range(chips)]
        for half in range(2)
        for core in range(CS)
    ]
    chip_groups = [[CS * chip + core for chip in range(CHIPS)] for core in range(CS)]

    own, give = choose(
        is_far,
        row,
        near_pieces,
        far_pieces,
    )
    give, qg_came = lax.optimization_barrier((give, qg_came))
    got = swap_dp(give)
    qg = lax.all_to_all(
        jnp.stack([qg_stay, qg_came], axis=1),
        "mp",
        split_axis=0,
        concat_axis=0,
        tiled=True,
        axis_index_groups=chip_lines,
    )
    span_shape = (CH_DEV, NBR * slice_len, E)
    own, got = own.reshape(span_shape), got.reshape(span_shape)
    neighbours = (own, got, swap(own, 1), swap(got, 1))

    result = attend(place, neighbours, (line_w, x_w, y_w, xy_mine, xy_came), qg)
    back = lax.all_to_all(
        result, "mp", split_axis=0, concat_axis=0, tiled=True, axis_index_groups=chip_groups
    )
    back = back.transpose(1, 2, 0, 3).reshape((2,) + queries.shape)
    return back[0], back[1]


def general(queries, cache, cache_scale, w_kv, nbr_shard, nbr_row, grad_out):
    dp_count = lax.axis_size("dp")
    mp_count = lax.axis_size("mp")
    my_mp = lax.axis_index("mp")
    slice_len = cache.shape[1]
    most_slots = 2 * ((dp_count * CH_DEV * NBR + mp_count - 1) // mp_count)
    local_query = lax.all_to_all(queries, "mp", split_axis=1, concat_axis=0, tiled=True)
    shard_blk, row_blk, slot_blk = requests(nbr_shard, nbr_row, dp_count, mp_count)
    to_me = shard_blk == my_mp
    slot_ids = jnp.arange(most_slots, dtype=jnp.int32)
    select = jnp.logical_and(to_me[:, None, :], slot_blk[:, None, :] == slot_ids[None, :, None])
    wanted = jnp.sum(jnp.where(select, row_blk[:, None, :], 0), axis=2)
    sending = (cache[wanted].astype(jnp.float32) * cache_scale[wanted][..., None]).astype(
        jnp.bfloat16
    )
    arrived = lax.all_to_all(sending, "mp", split_axis=0, concat_axis=0, tiled=True)
    flat_pieces = arrived.reshape(mp_count * most_slots, slice_len, E)
    own_shards = lax.dynamic_index_in_dim(shard_blk, my_mp, 0, keepdims=False)
    own_slots = lax.dynamic_index_in_dim(slot_blk, my_mp, 0, keepdims=False)
    pieces = jnp.take(flat_pieces, own_shards * most_slots + own_slots, axis=0)
    pieces = pieces.reshape(dp_count, CH_DEV * NBR, slice_len, E)
    gathered = lax.all_to_all(pieces, "dp", split_axis=0, concat_axis=2, tiled=True)
    neighbours = gathered.reshape(CH_DEV, NBR * NT, E)
    gathered_weights = lax.all_gather(w_kv, ("dp", "mp"), axis=0, tiled=False)
    all_weights = (
        gathered_weights.reshape((dp_count, mp_count) + w_kv.shape)
        .transpose(2, 1, 3, 0, 4)
        .reshape(2, E, HEADS * HEAD_DIM)
    )
    key_value = jnp.einsum(
        "cte,ken->kctn", neighbours, all_weights, preferred_element_type=jnp.float32
    ).astype(jnp.bfloat16)
    key_rows = key_value[0].reshape(CH_DEV, NBR * NT, HEADS, HEAD_DIM)
    values = key_value[1].reshape(CH_DEV, NBR * NT, HEADS, HEAD_DIM)
    query_c = local_query.reshape(HEADS, HEAD_DIM, CH_DEV, SPAN)
    affinity_logits = (
        jnp.einsum("hdcq,ckhd->chqk", query_c, key_rows, preferred_element_type=jnp.float32)
        * SCORE_SCALE
    )
    row_max = jnp.max(affinity_logits, axis=3, keepdims=True)
    exponent = jnp.exp(affinity_logits - row_max)
    attn_probs = exponent / jnp.sum(exponent, axis=3, keepdims=True)
    probs_low = attn_probs.astype(jnp.bfloat16)
    output_c = jnp.einsum(
        "chqk,ckhd->hdcq", probs_low, values, preferred_element_type=jnp.float32
    ).astype(jnp.bfloat16)
    output_rows = output_c.reshape(HEADS * HEAD_DIM, CH_DEV * SPAN)
    output_back = lax.all_to_all(output_rows, "mp", split_axis=0, concat_axis=1, tiled=True)
    local_grad = lax.all_to_all(grad_out, "mp", split_axis=1, concat_axis=0, tiled=True)
    grad_c = local_grad.reshape(HEADS, HEAD_DIM, CH_DEV, SPAN)
    dprobs = jnp.einsum("hdcq,ckhd->chqk", grad_c, values, preferred_element_type=jnp.float32)
    row_delta = jnp.einsum("hdcq,hdcq->chq", grad_c, output_c, preferred_element_type=jnp.float32)
    dscores = (attn_probs * (dprobs - row_delta[..., None]) * SCORE_SCALE).astype(jnp.bfloat16)
    grad_query = jnp.einsum(
        "chqk,ckhd->hdcq", dscores, key_rows, preferred_element_type=jnp.float32
    ).astype(jnp.bfloat16)
    grad_rows = grad_query.reshape(HEADS * HEAD_DIM, CH_DEV * SPAN)
    grad_back = lax.all_to_all(grad_rows, "mp", split_axis=0, concat_axis=1, tiled=True)
    return (output_back, grad_back)


def solution(mesh):
    fits = mesh.shape["dp"] == 2 and mesh.shape["mp"] == len(ALL)
    return jax.shard_map(
        small if fits else general,
        mesh=mesh,
        in_specs=(
            P("mp", "dp"),
            P("mp", "dp", None),
            P("mp", "dp"),
            P(None, "mp", "dp"),
            P(),
            P(),
            P("mp", "dp"),
        ),
        out_specs=(P("mp", "dp"), P("mp", "dp")),
        check_vma=False,
    )
```
